32 devices in a mesh: gx: 8 (over y, x, core), gy: 4 (over z).
Axes of the slice: x: 2, y: 2, z: 4, core: 2. Of those that a mesh axis runs over, the one named last changes fastest.
Arguments:
- gradient: bfloat16 [256, 256, 512], P(None, 'gx', 'gy'), may hold values from -6 to 6
- vertical: bfloat16 [4, 256, 256], replicated, may hold values from -0.375 to 0.375
- kernel: bfloat16 [64, 64], replicated, may hold values from -0.75 to 0.75
Outputs:
- increment: bfloat16 [256, 256, 512], P(None, 'gx', 'gy')
The draws below stay inside these ranges and needn't reach their ends.
All inputs are finite; a program needn't handle non-finite values.
Results may differ from the reference program's by a relative error of at most 0.0085.
Values may be sent and summed in bfloat16 or wider, within the bound.
No kernel may reach another device: no remote copies, remote signals or barrier semaphores. Data moves between devices by JAX's collectives and lax.ppermute only.
A program may use at most 64 MiB of HBM per device.

```python
import jax
import jax.numpy as jnp

FL = 256
NX = 256
NY = 512
NY3 = 64


def block_scale(key, shape, shards, smallest, largest):
    loudness = 1.0
    for dim, blocks in shards:
        draws = jax.random.uniform(jax.random.fold_in(jax.random.fold_in(key, 6), dim), (blocks,), jnp.float32, smallest / len(shards), largest / len(shards))
        loudness = loudness * jnp.repeat(jnp.exp(draws), shape[dim] // blocks).reshape((-1,) + (1,) * (len(shape) - 1 - dim))
    return loudness


def noise(key, shape, scale, bound, shards=(), dtype=jnp.bfloat16):
    drawn = scale * jax.random.normal(key, shape, jnp.float32)
    if shards:
        drawn = drawn * block_scale(key, shape, shards, -0.22, 0.18)
    return jnp.clip(drawn, -bound, bound).astype(dtype)


def setup_inputs(seed: int = 0) -> dict:
    keys = jax.random.split(jax.random.key(seed), 4)
    return {
        "gradient": noise(keys[0], (FL, NX, NY), 1.0, 6.0, ((1, 8), (2, 4))),
        "vertical": noise(keys[1], (4, FL, FL), FL ** -0.5, 0.375),
        "kernel": noise(keys[2], (NY3, NY3), NY3 ** -0.5, 0.75),
    }


def restrict_x(v):
    prev = jnp.roll(v, 1, axis=1)
    return v[:, 0::2, :] + 0.5 * (prev[:, 0::2, :] + v[:, 1::2, :])


def restrict_y(v):
    prev = jnp.concatenate([jnp.zeros_like(v[:, :, :1]), v[:, :, :-1]], axis=2)
    return v[:, :, 0::2] + 0.5 * (prev[:, :, 0::2] + v[:, :, 1::2])


def prolong_x(c):
    after = jnp.roll(c, -1, axis=1)
    odd = 0.5 * (c + after)
    return jnp.stack([c, odd], axis=2).reshape(c.shape[0], 2 * c.shape[1], c.shape[2])


def prolong_y(c):
    after = jnp.concatenate([c[:, :, 1:], jnp.zeros_like(c[:, :, :1])], axis=2)
    odd = 0.5 * (c + after)
    return jnp.stack([c, odd], axis=3).reshape(c.shape[0], c.shape[1], 2 * c.shape[2])


def mixing(matrix, field):
    width = field.shape[0]
    flat = jnp.dot(matrix, field.reshape(width, -1), preferred_element_type=jnp.float32)
    return flat.reshape(field.shape)


def reference(gradient, vertical, kernel):
    levels = [gradient]
    current = gradient
    for level in range(3):
        coarser = restrict_y(restrict_x(current.astype(jnp.float32))) / 1.5
        current = coarser.astype(jnp.bfloat16)
        levels.append(current)
    coarse = mixing(vertical[3], levels[3]).astype(jnp.bfloat16)
    width, rows, cols = coarse.shape
    spread = jnp.dot(coarse.reshape(width * rows, cols), kernel, preferred_element_type=jnp.float32)
    carry = (coarse.astype(jnp.float32) + spread.reshape(width, rows, cols)).astype(jnp.bfloat16)
    for level in (2, 1, 0):
        finer = prolong_y(prolong_x(carry.astype(jnp.float32)))
        carry = (mixing(vertical[level], levels[level]) + finer / 1.5).astype(jnp.bfloat16)
    return carry
```

```python
import jax
import jax.numpy as jnp
import ml_dtypes
import numpy as np
from jax import lax
from jax.experimental import pallas as pl
from jax.experimental.pallas import tpu as pltpu
from jax.sharding import PartitionSpec as P

BF16 = jnp.bfloat16
F32 = jnp.float32
HALF = 16
VMEM = pltpu.VMEM


def hat(level, fine, cell):
    size = 2**level
    return np.maximum(0.0, 1.0 - np.abs(fine - size * cell) / size)


def weights(level, xs, ys, cell_x, cell_y):
    wx = hat(level, np.asarray(xs)[:, None], np.asarray(cell_x)[None, :])
    wy = hat(level, np.asarray(ys)[:, None], np.asarray(cell_y)[None, :])
    return (wx[:, None, :] * wy[None, :, :]).reshape(len(xs) * len(ys), len(cell_x))


def up16(n):
    return -(-n // 16) * 16


class Plan:
    def __init__(self, rows, cols):
        self.rows, self.cols = rows, cols
        ys = range(cols)
        counts = [(rows >> k, cols >> k) for k in range(4)]
        self.counts = counts
        row_cells = [(k, c) for k in (1, 2, 3) for c in range(counts[k][1] + 1)]
        self.row_cells = row_cells
        self.row_size = up16(len(row_cells))
        assert self.row_size == 128
        n3, m3 = counts[3][0] + 1, counts[3][1] + 1
        self.block = up16(n3 * m3)
        self.edge = (n3 * m3) // 16 * 16
        self.spare = n3 * m3 - self.edge
        level3 = [(3, r, c) for r in range(n3) for c in range(m3)]
        edge = [(k, r) for k in (1, 2) for r in range(counts[k][0] + 1)]
        right = level3 + [(k, r, counts[k][1]) for k, r in edge]
        left = level3 + [(k, r, 0) for k, r in edge]
        self.message = up16(len(right))
        self.edge_size = self.message - self.edge
        cells = []
        for part in (right, left):
            cells += part + [None] * (self.message - len(part))
        self.column_cells = cells

        def table(cells, xs):
            out = np.zeros((len(cells), len(xs) * cols))
            for k in (1, 2, 3):
                where = [i for i, cell in enumerate(cells) if cell is not None and cell[0] == k]
                at = [cells[i] for i in where]
                out[where] = weights(k, xs, ys, [c[1] for c in at], [c[2] for c in at]).T
            return out

        pad = [None] * (self.row_size - len(row_cells))
        lower = [(k, 0, c) for k, c in row_cells] + pad
        upper = [(k, counts[k][0], c) for k, c in row_cells] + pad
        self.send_lower = table(lower, range(0, 8))
        self.send_upper = table(upper, range(rows - 8, rows))
        self.send_column = table(cells, range(rows))
        merge = np.zeros((len(cells), 2 * self.row_size))
        for i, cell in enumerate(cells):
            if cell is None:
                continue
            k, r, c = cell
            if r == 0:
                merge[i, row_cells.index((k, c))] = 1
            if r == counts[k][0]:
                merge[i, self.row_size + row_cells.index((k, c))] = 1
        self.merge = merge
        c1, c2 = counts[1][1], counts[2][1]
        grid = lambda n, m: (np.repeat(np.arange(n), m), np.tile(np.arange(m), n))
        self.to_level1 = weights(1, range(-1, 8), ys, *grid(4, c1))
        self.to_level2 = weights(1, range(counts[1][0]), range(c1), *grid(counts[2][0], c2))
        self.even = weights(1, range(0, 2), ys, *grid(2, c1)).T
        self.odd = weights(1, range(2, 4), ys, *grid(4, c1)).T
        def from_row(xs, ends):
            out = np.zeros((2 * self.row_size, 4 * cols))
            for i, (k, c) in enumerate(row_cells):
                if k < 3 and c < counts[k][1]:
                    out[(k - 1) * self.row_size + i] = weights(k, xs, ys, [ends[k]], [c])[:, 0]
            return out

        self.from_first = from_row(range(0, 4), (0, 0, 0))
        self.from_last = from_row(range(rows - 4, rows), [n for n, _ in counts])
        final = [c for c in level3] + [None] * (self.block - len(level3))
        for k in (1, 2):
            for side in (0, 1):
                part = [None] * self.spare
                for level, r in edge:
                    part.append((k, r, side * counts[k][1]) if level == k else None)
                final += part + [None] * (self.edge_size - len(part))
        self.final_size = len(final)
        self.final = table(final, range(rows))


def const(table):
    return jnp.asarray(np.asarray(table).astype(ml_dtypes.bfloat16))


def in_vmem(x):
    return pltpu.with_memory_space_constraint(x, VMEM)


def dot(a, b):
    return jnp.dot(a, b, preferred_element_type=F32)


def dot_nt(a, b):
    return lax.dot_general(a, b, (((1,), (1,)), ((), ())), preferred_element_type=F32)


def first_kernel(plan, x_ref, lower_ref, upper_ref, flat_ref, a_ref, b_ref, buf, nat, sem):
    rows, cols = plan.rows, plan.cols
    width = x_ref.shape[0]
    parts = rows // HALF
    copies = [
        pltpu.make_async_copy(x_ref.at[:, pl.ds(h * HALF, HALF), :], buf.at[h], sem.at[h])
        for h in range(parts)
    ]
    for copy in copies:
        copy.start()
    even = lax.rem(lax.axis_index("gx"), 2) == 0

    def message(table_ref, start):
        total = None
        for j in range(4):
            lanes = pl.ds((start + 2 * j) * cols, 2 * cols)
            term = dot_nt(table_ref[:, pl.ds(2 * j * cols, 2 * cols)], flat_ref[:, lanes])
            total = term if total is None else total + term
        return total.astype(BF16)

    low = None
    for h in range(parts):
        copies[h].wait()
        nat[h] = buf[h].astype(F32).reshape(width * HALF, cols)
        for x in range(HALF):
            row = nat[h, pl.ds(x, width, stride=HALF), :]
            flat_ref[:, pl.ds((h * HALF + x) * cols, cols)] = row.astype(BF16)
        if h == 0:
            low = message(lower_ref, 0)
    up = message(upper_ref, rows - 8)
    a_ref[...] = jnp.where(even, up, low)
    b_ref[...] = jnp.where(even, low, up)


def column_kernel(plan, flat_ref, table_ref, out_ref):
    total = None
    for j in range(plan.rows // 2):
        lanes = pl.ds(2 * j * plan.cols, 2 * plan.cols)
        term = dot_nt(table_ref[:, lanes], flat_ref[:, lanes])
        total = term if total is None else total + term
    out_ref[...] = total


def merge_kernel(plan, own_ref, a_ref, b_ref, merge_ref, right_ref, left_ref, block_ref):
    even = lax.rem(lax.axis_index("gx"), 2) == 0
    size = plan.row_size
    a, b = a_ref[...], b_ref[...]
    before, after = jnp.where(even, b, a), jnp.where(even, a, b)
    total = own_ref[...] + dot(merge_ref[:, :size], before) + dot(merge_ref[:, size:], after)
    total = total.astype(BF16)
    right_ref[...] = total[: plan.message]
    left_ref[...] = total[plan.message :]
    block_ref[...] = total[: plan.block]


def local_kernel(
    plan, count, flat_ref, v_ref, k_ref, sa_ref, sb_ref, ra_ref, rb_ref, t1_ref, t2_ref, u2_ref, even_ref, odd_ref,
    first_ref, last_ref, base_ref, spread_ref, keep_ref, level1, carry1,
):
    rows, cols = plan.rows, plan.cols
    c1 = plan.counts[1][1]
    n1 = plan.counts[1][0]
    for k in range(rows // 8):
        total = None
        for j in range(4):
            lanes = pl.ds((8 * k + 2 * j) * cols, 2 * cols)
            term = dot(flat_ref[:, lanes], t1_ref[pl.ds((2 * j + 1) * cols, 2 * cols), :])
            total = term if total is None else total + term
        if k > 0:
            total = total + dot(flat_ref[:, pl.ds((8 * k - 1) * cols, cols)], t1_ref[pl.ds(0, cols), :])
        level1[:, pl.ds(4 * k * c1, 4 * c1)] = (total * (1 / 1.5)).astype(BF16)
    level2 = (dot(level1[...], t2_ref[...]) * (1 / 1.5)).astype(BF16)
    mixed2 = (dot(v_ref[2], level2) * (1 / 1.5)).astype(BF16)
    step = 4 * c1
    for k in range(n1 * c1 // step):
        lanes = pl.ds(k * step, step)
        mixed1 = dot(v_ref[1], level1[:, lanes]) + dot(mixed2, u2_ref[:, lanes])
        carry1[:, lanes] = (mixed1 * (1 / 1.5)).astype(BF16)

    even = lax.rem(lax.axis_index("gx"), 2) == 0
    a, b = ra_ref[...], rb_ref[...]
    before, after = jnp.where(even, b, a), jnp.where(even, a, b)
    own = jnp.where(even, sa_ref[...], sb_ref[...])
    after = (after.astype(F32) + own.astype(F32)).astype(BF16)

    def mixed_rows(message):
        one = dot_nt(v_ref[1], message) * (1 / 1.5**2)
        two = dot_nt(v_ref[2], message) * (1 / 1.5**4)
        return jnp.concatenate([one, two], axis=1).astype(BF16)

    first, last = mixed_rows(before), mixed_rows(after)
    pairs = rows // 2
    for i in range(pairs):
        lanes = pl.ds(2 * i * cols, 2 * cols)
        total = dot(v_ref[0], flat_ref[:, lanes])
        if i % 2 == 0:
            total = total + dot(carry1[:, pl.ds(i * c1, 2 * c1)], even_ref[...])
        elif i < pairs - 1:
            total = total + dot(carry1[:, pl.ds((i - 1) * c1, 4 * c1)], odd_ref[...])
        else:
            total = total + dot(carry1[:, pl.ds((i - 1) * c1, 2 * c1)], odd_ref[pl.ds(0, 2 * c1), :])
        if i < 2:
            total = total + dot(first, first_ref[:, pl.ds(2 * i * cols, 2 * cols)])
        if i >= pairs - 2:
            total = total + dot(last, last_ref[:, pl.ds(2 * (i - pairs + 2) * cols, 2 * cols)])
        base_ref[:, lanes] = total

    n3, m3 = plan.counts[3][0] + 1, plan.counts[3][1] + 1
    size = k_ref.shape[0]
    block = plan.block
    z = lax.axis_index("gy")

    def parts(shape, dim):
        index = lax.broadcasted_iota(jnp.int32, shape, dim)
        row = jnp.zeros(shape, jnp.int32)
        for r in range(1, n3 + 1):
            row = row + jnp.where(index >= r * m3, 1, 0)
        return row, index - row * m3

    def one(mask):
        return jnp.where(mask, 1.0, 0.0).astype(BF16)

    row, col = parts((block, size), 0)
    place = lax.broadcasted_iota(jnp.int32, (block, size), 1)
    pick = one((place == z * (m3 - 1) + col) & (row < n3))
    picked = dot_nt(pick, k_ref[...]).astype(BF16)
    target_row, target_col = parts((block, block), 0)
    source_row, source_col = parts((block, block), 1)
    same = (target_row == source_row) & (target_row < n3)
    target = z * (m3 - 1) + target_col
    _, col = parts((size, block), 1)
    place = lax.broadcasted_iota(jnp.int32, (size, block), 0)
    for d in range(count):
        start = lax.rem(z - d + count, count) * (m3 - 1)
        spread = dot(picked, one(place == start + col))
        lanes = pl.ds(d * block, block)
        spread_ref[d] = jnp.where(same, spread, 0.0).astype(BF16)
        keep_ref[d] = one(same & (target == start + source_col) & (target < size))


def last_kernel(plan, count, *refs):
    own_ref, *in_refs = refs[: count]
    v_ref, spread_ref, keep_ref, final_ref, base_ref, out_ref, nat, buf, sem = refs[count:]
    rows, cols = plan.rows, plan.cols
    width = v_ref.shape[1]
    block = plan.block
    z = lax.axis_index("gy")
    carry = None
    for d in range(count):
        level3 = own_ref[:block] if d == 0 else in_refs[d - 1][:block]
        mixed = (dot_nt(level3, v_ref[3]) * (1 / 1.5**3)).astype(BF16)
        term = dot(spread_ref[d], mixed) + dot(keep_ref[d], mixed)
        carry = term if carry is None else carry + term
    carry = carry.astype(BF16).astype(F32) * (1 / 1.5**3)
    left = in_refs[0][plan.edge :]
    right = (in_refs[-1][plan.edge :].astype(F32) + own_ref[plan.edge :].astype(F32)).astype(BF16)
    left = jnp.where(z > 0, left, jnp.zeros_like(left))
    right = jnp.where(z < count - 1, right, jnp.zeros_like(right))
    edges = jnp.concatenate([left, right], axis=0)
    one = dot_nt(edges, v_ref[1]) * (1 / 1.5**2)
    two = dot_nt(edges, v_ref[2]) * (1 / 1.5**4)
    parts = jnp.concatenate([carry, one, two], axis=0).T.astype(BF16)
    copies = []
    for h in range(rows // HALF):
        for x in range(0, HALF, 2):
            lanes = pl.ds((h * HALF + x) * cols, 2 * cols)
            total = base_ref[:, lanes] + dot(parts, final_ref[:, lanes])
            nat[h, pl.ds(x, width, stride=HALF), :] = total[:, :cols]
            nat[h, pl.ds(x + 1, width, stride=HALF), :] = total[:, cols:]
        buf[h] = nat[h].reshape(width, HALF, cols).astype(BF16)
        copy = pltpu.make_async_copy(buf.at[h], out_ref.at[:, pl.ds(h * HALF, HALF), :], sem.at[h])
        copy.start()
        copies.append(copy)
    for copy in copies:
        copy.wait()


LIMIT = 48 * 1024 * 1024


def call(kernel, ins, outs, scratch=(), any_in=(), any_out=(), name=None, cost=None):
    specs = [pl.BlockSpec(memory_space=pl.ANY if i in any_in else VMEM) for i in range(len(ins))]
    out_specs = [pl.BlockSpec(memory_space=pl.ANY if i in any_out else VMEM) for i in range(len(outs))]
    out_shape = [
        jax.ShapeDtypeStruct(s, t) if i in any_out else VMEM(s, t) for i, (s, t) in enumerate(outs)
    ]
    ins = [x if i in any_in else in_vmem(x) for i, x in enumerate(ins)]
    return pl.pallas_call(
        kernel,
        in_specs=specs,
        out_specs=out_specs,
        out_shape=out_shape,
        scratch_shapes=list(scratch),
        compiler_params=pltpu.CompilerParams(vmem_limit_bytes=LIMIT),
        cost_estimate=cost,
        name=name,
    )(*ins)


def solution(mesh):
    across, along = mesh.shape["gx"], mesh.shape["gy"]

    def swap(x, first):
        def partner(i):
            return i ^ 1 if first else (i + 1 if i % 2 else i - 1) % across

        return lax.ppermute(x, "gx", [(i, partner(i)) for i in range(across)])

    def on_device(gradient, vertical, kernel):
        width, rows, cols = gradient.shape
        plan = Plan(rows, cols)
        parts = rows // HALF
        size = rows * cols
        flat, send_a, send_b = call(
            lambda *refs: first_kernel(plan, *refs),
            [gradient, const(plan.send_lower), const(plan.send_upper)],
            [((width, size), BF16), ((plan.row_size, width), BF16), ((plan.row_size, width), BF16)],
            [
                VMEM((parts, width, HALF, cols), BF16),
                VMEM((parts, width * HALF, cols), F32),
                pltpu.SemaphoreType.DMA((parts,)),
            ],
            any_in=(0,),
            name="first",
        )
        recv_a, recv_b = swap(send_a, True), swap(send_b, False)
        cells = 2 * plan.message
        (own,) = call(
            lambda *refs: column_kernel(plan, *refs),
            [flat, const(plan.send_column)],
            [((cells, width), F32)],
            name="columns",
            cost=pl.CostEstimate(flops=2 * cells * width * size, bytes_accessed=4 * 1024 * 1024, transcendentals=0),
        )
        right, left, block = call(
            lambda *refs: merge_kernel(plan, *refs),
            [own, recv_a, recv_b, const(plan.merge)],
            [((plan.message, width), BF16), ((plan.message, width), BF16), ((plan.block, width), BF16)],
            name="merge",
        )
        messages = [block] * (along + 1)
        messages[1], messages[along - 1] = right, left
        arrived = [
            lax.ppermute(messages[d], "gy", [(i, (i + d) % along) for i in range(along)]) for d in range(1, along)
        ]
        base, spread, keep = call(
            lambda *refs: local_kernel(plan, along, *refs),
            [
                flat, vertical, kernel, send_a, send_b, recv_a, recv_b, const(plan.to_level1), const(plan.to_level2),
                const(plan.to_level2.T), const(plan.even), const(plan.odd), const(plan.from_first),
                const(plan.from_last),
            ],
            [
                ((width, size), F32),
                ((along, plan.block, plan.block), BF16),
                ((along, plan.block, plan.block), BF16),
            ],
            [VMEM((width, size // 4), BF16), VMEM((width, size // 4), BF16)],
            name="local",
            cost=pl.CostEstimate(flops=6 * width * width * size, bytes_accessed=8 * 1024 * 1024, transcendentals=0),
        )
        (out,) = call(
            lambda *refs: last_kernel(plan, along, *refs),
            [right, *arrived, vertical, spread, keep, const(plan.final), base],
            [((width, rows, cols), BF16)],
            [
                VMEM((parts, width * HALF, cols), F32),
                VMEM((parts, width, HALF, cols), BF16),
                pltpu.SemaphoreType.DMA((parts,)),
            ],
            any_out=(0,),
            name="last",
        )
        return out

    spec = P(None, "gx", "gy")
    return jax.shard_map(on_device, mesh=mesh, in_specs=(spec, P(), P()), out_specs=spec, check_vma=False)
```

```python
import jax
import jax.numpy as jnp
import ml_dtypes
import numpy as np
from jax import lax
from jax.experimental import pallas as pl
from jax.experimental.pallas import tpu as pltpu
from jax.sharding import PartitionSpec as P

BF16 = jnp.bfloat16
F32 = jnp.float32
HALF = 16
CHUNKS = 2
VMEM = pltpu.VMEM


def hat(level, fine, cell):
    size = 2**level
    return np.maximum(0.0, 1.0 - np.abs(fine - size * cell) / size)


def weights(level, xs, ys, cell_x, cell_y):
    wx = hat(level, np.asarray(xs)[:, None], np.asarray(cell_x)[None, :])
    wy = hat(level, np.asarray(ys)[:, None], np.asarray(cell_y)[None, :])
    return (wx[:, None, :] * wy[None, :, :]).reshape(len(xs) * len(ys), len(cell_x))


def up16(n):
    return -(-n // 16) * 16


class Plan:
    def __init__(self, rows, cols):
        self.rows, self.cols = rows, cols
        ys = range(cols)
        counts = [(rows >> k, cols >> k) for k in range(4)]
        self.counts = counts
        row_cells = [(k, c) for k in (1, 2, 3) for c in range(counts[k][1] + 1)]
        self.row_cells = row_cells
        self.row_size = up16(len(row_cells))
        assert self.row_size == 128
        n3, m3 = counts[3][0] + 1, counts[3][1] + 1
        self.cells3 = up16(n3 * m3)
        self.block = -(-n3 * m3 // 128) * 128
        self.edge = (n3 * m3) // 16 * 16
        self.spare = n3 * m3 - self.edge
        level3 = [(3, r, c) for r in range(n3) for c in range(m3)]
        edge = [(k, r) for k in (1, 2) for r in range(counts[k][0] + 1)]
        self.message = up16(len(level3) + len(edge))
        self.edge_size = self.message - self.edge
        cells = []
        for side in (1, 0):
            part = [(k, r, side * counts[k][1]) for k, r in edge]
            part = (level3[self.edge :] if side else [None] * self.spare) + part
            cells += (level3[: self.edge] if side else []) + part + [None] * (self.edge_size - len(part))
        cells += [None] * (-len(cells) % 16)
        self.cells = len(cells)

        def table(cells, xs):
            out = np.zeros((len(cells), len(xs) * cols))
            for k in (1, 2, 3):
                where = [i for i, cell in enumerate(cells) if cell is not None and cell[0] == k]
                at = [cells[i] for i in where]
                out[where] = weights(k, xs, ys, [c[1] for c in at], [c[2] for c in at]).T
            return out

        self.send_column = table(cells, range(rows))
        merge = np.zeros((len(cells), 2 * self.row_size))
        for i, cell in enumerate(cells):
            if cell is None:
                continue
            k, r, c = cell
            if r == 0:
                merge[i, row_cells.index((k, c))] = 1
            if r == counts[k][0]:
                merge[i, self.row_size + row_cells.index((k, c))] = 1
        self.merge = merge
        c1, c2 = counts[1][1], counts[2][1]
        grid = lambda n, m: (np.repeat(np.arange(n), m), np.tile(np.arange(m), n))
        self.to_level1 = weights(1, range(-1, 8), ys, *grid(4, c1))
        self.to_level2 = weights(1, range(counts[1][0]), range(c1), *grid(counts[2][0], c2))
        self.even = weights(1, range(0, 2), ys, *grid(2, c1)).T
        self.odd = weights(1, range(2, 4), ys, *grid(4, c1)).T
        def from_row(xs, ends):
            out = np.zeros((2 * self.row_size, 4 * cols))
            for i, (k, c) in enumerate(row_cells):
                if k < 3 and c < counts[k][1]:
                    out[(k - 1) * self.row_size + i] = weights(k, xs, ys, [ends[k]], [c])[:, 0]
            return out

        self.from_first = from_row(range(0, 4), (0, 0, 0))
        self.from_last = from_row(range(rows - 4, rows), [n for n, _ in counts])
        final = [c for c in level3] + [None] * (self.block - len(level3))
        for k in (1, 2):
            for side in (0, 1):
                part = [None] * self.spare
                for level, r in edge:
                    part.append((k, r, side * counts[k][1]) if level == k else None)
                final += part + [None] * (self.edge_size - len(part))
        self.final_size = len(final)
        self.final = table(final, range(rows))


def const(table):
    return jnp.asarray(np.asarray(table).astype(ml_dtypes.bfloat16))


def dot(a, b):
    return jnp.dot(a, b, preferred_element_type=F32)


def dot_nt(a, b):
    return lax.dot_general(a, b, (((1,), (1,)), ((), ())), preferred_element_type=F32)


def row_table(plan, x, end):
    shape = (plan.row_size, plan.cols)
    cell = lax.broadcasted_iota(jnp.int32, shape, 0)
    y = lax.broadcasted_iota(jnp.int32, shape, 1)
    start, scale, inverse, used = cell * 0, cell * 0, jnp.zeros(shape, F32), 0
    for k in (1, 2, 3):
        stop = used + plan.counts[k][1] + 1
        mine = (cell >= used) & (cell < stop)
        start = jnp.where(mine, used, start)
        scale = jnp.where(mine, 2**k, scale)
        inverse = jnp.where(mine, 0.5**k, inverse)
        used = stop
    along = jnp.maximum(0, scale - jnp.abs(y - scale * (cell - start))).astype(F32)
    across = jnp.maximum(0, scale - abs(x - end)).astype(F32)
    return (along * across * (inverse * inverse)).astype(BF16)


def first_kernel(plan, x_ref, *refs):
    count = (len(refs) - 6) // 2
    fetched = refs[:count]
    raw_ref, flat_ref, a_ref, b_ref = refs[count : count + 4]
    nat, sem = refs[-2:]
    rows, cols = plan.rows, plan.cols
    width = x_ref.shape[0]
    chunk = width // CHUNKS
    last = rows // HALF - 1
    copies = {}
    for h in range(last + 1):
        for c in range(CHUNKS):
            fields = pl.ds(c * chunk, chunk)
            copies[h, c] = pltpu.make_async_copy(
                x_ref.at[fields, pl.ds(h * HALF, HALF), :], raw_ref.at[h, fields], sem.at[h, c]
            )
            copies[h, c].start()
    fetches = [
        pltpu.make_async_copy(src, dst, sem.at[last + 1, i])
        for i, (src, dst) in enumerate(zip(fetched, refs[count + 4 : -2]))
    ]
    for fetch in fetches:
        fetch.start()
    even = lax.rem(lax.axis_index("gx"), 2) == 0

    def message(h, start, end):
        for c in range(CHUNKS):
            copies[h, c].wait()
            fields = pl.ds(c * chunk, chunk)
            nat[c] = raw_ref[h, fields].astype(F32)[:, start : start + 8, :].reshape(chunk * 8, cols)
            for x in range(8):
                lanes = pl.ds(((8 if start else 0) + x) * cols, cols)
                flat_ref[fields, lanes] = nat[c, pl.ds(x, chunk, stride=8), :].astype(BF16)
        total = None
        for x in range(0, 8, 2):
            table = jnp.concatenate([row_table(plan, x, end), row_table(plan, x + 1, end)], axis=1)
            term = dot_nt(table, flat_ref[:, pl.ds(((8 if start else 0) + x) * cols, 2 * cols)])
            total = term if total is None else total + term
        return total.astype(BF16)

    low = message(0, 0, 0)
    up = message(last, HALF - 8, 8)
    a_ref[...] = jnp.where(even, up, low)
    b_ref[...] = jnp.where(even, low, up)
    for h in range(1, last):
        for c in range(CHUNKS):
            copies[h, c].wait()
    for fetch in fetches:
        fetch.wait()


class Rows:
    def __init__(self, plan, ends_ref, inner_ref):
        self.plan, self.ends, self.inner = plan, ends_ref, inner_ref

    def __call__(self, x, count):
        rows, cols = self.plan.rows, self.plan.cols
        if x < 8:
            return self.ends[:, pl.ds(x * cols, count * cols)]
        if x >= rows - 8:
            return self.ends[:, pl.ds((x - rows + 16) * cols, count * cols)]
        return self.inner[:, pl.ds((x - 8) * cols, count * cols)]


def inner_kernel(
    plan, raw_ref, ends_ref, v_ref, column_ref, t1_ref, t2_ref, inner_ref, own_ref, carry1_ref, nat, level1
):
    rows, cols = plan.rows, plan.cols
    width = ends_ref.shape[0]
    for h in range(rows // HALF):
        nat[h] = raw_ref[h].astype(F32).reshape(width * HALF, cols)
        for x in range(HALF):
            at = h * HALF + x
            if 8 <= at < rows - 8:
                row = nat[h, pl.ds(x, width, stride=HALF), :]
                inner_ref[:, pl.ds((at - 8) * cols, cols)] = row.astype(BF16)
    fine = Rows(plan, ends_ref, inner_ref)
    total = None
    for x in range(0, rows, 2):
        term = dot_nt(column_ref[:, pl.ds(x * cols, 2 * cols)], fine(x, 2))
        total = term if total is None else total + term
    own_ref[...] = total
    n1, c1 = plan.counts[1]
    for k in range(rows // 8):
        total = None
        for j in range(4):
            term = dot(fine(8 * k + 2 * j, 2), t1_ref[pl.ds((2 * j + 1) * cols, 2 * cols), :])
            total = term if total is None else total + term
        if k > 0:
            total = total + dot(fine(8 * k - 1, 1), t1_ref[pl.ds(0, cols), :])
        level1[:, pl.ds(4 * k * c1, 4 * c1)] = (total * (1 / 1.5)).astype(BF16)
    level2 = (dot(level1[...], t2_ref[...]) * (1 / 1.5)).astype(BF16)
    mixed2 = (dot(v_ref[2], level2) * (1 / 1.5)).astype(BF16)
    step = 4 * c1
    for k in range(n1 * c1 // step):
        lanes = pl.ds(k * step, step)
        mixed1 = dot(v_ref[1], level1[:, lanes]) + dot_nt(mixed2, t2_ref[lanes, :])
        carry1_ref[:, lanes] = (mixed1 * (1 / 1.5)).astype(BF16)


def merge_kernel(plan, own_ref, a_ref, b_ref, merge_ref, right_ref, left_ref, block_ref):
    even = lax.rem(lax.axis_index("gx"), 2) == 0
    size = plan.row_size
    a, b = a_ref[...], b_ref[...]
    before, after = jnp.where(even, b, a), jnp.where(even, a, b)
    total32 = own_ref[...] + dot(merge_ref[:, :size], before) + dot(merge_ref[:, size:], after)
    total = total32.astype(BF16)
    right_ref[...] = total[: plan.message]
    left_ref[: plan.edge] = total[: plan.edge]
    row = lax.broadcasted_iota(jnp.int32, (plan.edge_size, total.shape[1]), 0)
    tile = jnp.where(row < plan.spare, total32[plan.edge : plan.message], total32[plan.message :])
    left_ref[plan.edge :] = tile.astype(BF16)
    block_ref[...] = total[: plan.cells3]


def local_kernel(
    plan, count, ends_ref, inner_ref, carry1, v_ref, k_ref, sa_ref, sb_ref, ra_ref, rb_ref, even_ref, odd_ref,
    first_ref, last_ref, base_ref, spread_ref,
):
    rows, cols = plan.rows, plan.cols
    n1, c1 = plan.counts[1]
    fine = Rows(plan, ends_ref, inner_ref)

    even = lax.rem(lax.axis_index("gx"), 2) == 0
    a, b = ra_ref[...], rb_ref[...]
    before, after = jnp.where(even, b, a), jnp.where(even, a, b)
    own = jnp.where(even, sa_ref[...], sb_ref[...])
    after = (after.astype(F32) + own.astype(F32)).astype(BF16)

    def mixed_rows(message):
        one = dot_nt(v_ref[1], message) * (1 / 1.5**2)
        two = dot_nt(v_ref[2], message) * (1 / 1.5**4)
        return jnp.concatenate([one, two], axis=1).astype(BF16)

    first, last = mixed_rows(before), mixed_rows(after)
    pairs = rows // 2
    for i in range(pairs):
        lanes = pl.ds(2 * i * cols, 2 * cols)
        total = dot(v_ref[0], fine(2 * i, 2))
        if i % 2 == 0:
            total = total + dot(carry1[:, pl.ds(i * c1, 2 * c1)], even_ref[...])
        elif i < pairs - 1:
            total = total + dot(carry1[:, pl.ds((i - 1) * c1, 4 * c1)], odd_ref[...])
        else:
            total = total + dot(carry1[:, pl.ds((i - 1) * c1, 2 * c1)], odd_ref[pl.ds(0, 2 * c1), :])
        if i < 2:
            total = total + dot(first, first_ref[:, pl.ds(2 * i * cols, 2 * cols)])
        if i >= pairs - 2:
            total = total + dot(last, last_ref[:, pl.ds(2 * (i - pairs + 2) * cols, 2 * cols)])
        base_ref[:, lanes] = total

    n3, m3 = plan.counts[3][0] + 1, plan.counts[3][1] + 1
    size = k_ref.shape[0]
    block, cells3 = plan.block, plan.cells3
    z = lax.axis_index("gy")

    def parts(shape, dim):
        index = lax.broadcasted_iota(jnp.int32, shape, dim)
        row = jnp.zeros(shape, jnp.int32)
        for r in range(1, n3 + 1):
            row = row + jnp.where(index >= r * m3, 1, 0)
        return row, index - row * m3

    def one(mask):
        return jnp.where(mask, 1.0, 0.0).astype(BF16)

    row, col = parts((size, block), 1)
    place = lax.broadcasted_iota(jnp.int32, (size, block), 0)
    picked = dot(k_ref[...], one((place == z * (m3 - 1) + col) & (row < n3))).astype(BF16)
    source_row, source_col = parts((cells3, block), 0)
    target_row, target_col = parts((cells3, block), 1)
    same = (target_row == source_row) & (target_row < n3)
    target = z * (m3 - 1) + target_col
    _, col = parts((cells3, size), 0)
    place = lax.broadcasted_iota(jnp.int32, (cells3, size), 1)
    for d in range(count):
        start = lax.rem(z - d + count, count) * (m3 - 1)
        spread = jnp.where(same, dot(one(place == start + col), picked), 0.0).astype(BF16)
        keep = one(same & (target == start + source_col) & (target < size))
        spread_ref[pl.ds(d * cells3, cells3), :block] = spread
        spread_ref[pl.ds(d * cells3, cells3), block:] = keep


def last_kernel(plan, count, *refs):
    own_ref, *in_refs = refs[:count]
    v_ref, spread_ref, final_ref, base_ref, out_ref, nat, buf, sem = refs[count:]
    rows, cols = plan.rows, plan.cols
    width = v_ref.shape[1]
    block = plan.block
    z = lax.axis_index("gy")
    level3 = jnp.concatenate([own_ref[: plan.cells3]] + [ref[: plan.cells3] for ref in in_refs], axis=0)
    mixed = (dot_nt(v_ref[3], level3) * (1 / 1.5**3)).astype(BF16)
    carry = dot(mixed, spread_ref[...])
    carry = (carry[:, :block] + carry[:, block:]) * (1 / 1.5**3)
    left = in_refs[0][plan.edge :]
    right = (in_refs[-1][plan.edge :].astype(F32) + own_ref[plan.edge :].astype(F32)).astype(BF16)
    left = jnp.where(z > 0, left, jnp.zeros_like(left))
    right = jnp.where(z < count - 1, right, jnp.zeros_like(right))
    edges = jnp.concatenate([left, right], axis=0)
    one = dot_nt(v_ref[1], edges) * (1 / 1.5**2)
    two = dot_nt(v_ref[2], edges) * (1 / 1.5**4)
    parts = jnp.concatenate([carry, one, two], axis=1).astype(BF16)
    copies = []
    for h in range(rows // HALF):
        for x in range(0, HALF, 2):
            lanes = pl.ds((h * HALF + x) * cols, 2 * cols)
            total = base_ref[:, lanes] + dot(parts, final_ref[:, lanes])
            nat[h, pl.ds(x, width, stride=HALF), :] = total[:, :cols]
            nat[h, pl.ds(x + 1, width, stride=HALF), :] = total[:, cols:]
        buf[h] = nat[h].reshape(width, HALF, cols).astype(BF16)
        copy = pltpu.make_async_copy(buf.at[h], out_ref.at[:, pl.ds(h * HALF, HALF), :], sem.at[h])
        copy.start()
        copies.append(copy)
    for copy in copies:
        copy.wait()


LIMIT = 14 * 1024 * 1024


def call(kernel, ins, outs, scratch=(), hbm=(), any_out=(), name=None, cost=None):
    specs = [pl.BlockSpec(memory_space=pl.ANY if i in hbm else VMEM) for i in range(len(ins))]
    out_specs = [pl.BlockSpec(memory_space=pl.ANY if i in any_out else VMEM) for i in range(len(outs))]
    out_shape = [
        jax.ShapeDtypeStruct(s, t) if i in any_out else VMEM(s, t) for i, (s, t) in enumerate(outs)
    ]
    ins = [pltpu.with_memory_space_constraint(x, pltpu.HBM if i in hbm else VMEM) for i, x in enumerate(ins)]
    return pl.pallas_call(
        kernel,
        in_specs=specs,
        out_specs=out_specs,
        out_shape=out_shape,
        scratch_shapes=list(scratch),
        compiler_params=pltpu.CompilerParams(vmem_limit_bytes=LIMIT),
        cost_estimate=cost,
        name=name,
    )(*ins)


def solution(mesh):
    across, along = mesh.shape["gx"], mesh.shape["gy"]

    def swap(x, first):
        def partner(i):
            return i ^ 1 if first else (i + 1 if i % 2 else i - 1) % across

        return lax.ppermute(x, "gx", [(i, partner(i)) for i in range(across)])

    def on_device(gradient, vertical, kernel):
        width, rows, cols = gradient.shape
        plan = Plan(rows, cols)
        parts = rows // HALF
        size = rows * cols
        row_message = ((plan.row_size, width), BF16)
        fetched = [vertical, const(plan.send_column), const(plan.to_level1), const(plan.to_level2)]
        raw, ends, send_a, send_b, vertical, column, to_level1, to_level2 = call(
            lambda *refs: first_kernel(plan, *refs),
            [gradient, *fetched],
            [((parts, width, HALF, cols), BF16), ((width, 16 * cols), BF16), row_message, row_message]
            + [(x.shape, x.dtype) for x in fetched],
            [VMEM((CHUNKS, width // CHUNKS * 8, cols), F32), pltpu.SemaphoreType.DMA((parts + 1, max(CHUNKS, 4)))],
            hbm=range(5),
            name="first",
        )
        recv_a, recv_b = swap(send_a, True), swap(send_b, False)
        cells = plan.cells
        inner, own, carry1 = call(
            lambda *refs: inner_kernel(plan, *refs),
            [
                raw, ends, vertical, column, to_level1, to_level2,
            ],
            [((width, size - 16 * cols), BF16), ((cells, width), F32), ((width, size // 4), BF16)],
            [VMEM((parts, width * HALF, cols), F32), VMEM((width, size // 4), BF16)],
            name="inner",
            cost=pl.CostEstimate(flops=3 * cells * width * size, bytes_accessed=4 * 1024 * 1024, transcendentals=0),
        )
        right, left, block = call(
            lambda *refs: merge_kernel(plan, *refs),
            [own, recv_a, recv_b, const(plan.merge)],
            [((plan.message, width), BF16), ((plan.message, width), BF16), ((plan.cells3, width), BF16)],
            name="merge",
        )
        messages = [block] * (along + 1)
        messages[1], messages[along - 1] = right, left
        arrived = [
            lax.ppermute(messages[d], "gy", [(i, (i + d) % along) for i in range(along)]) for d in range(1, along)
        ]
        base, spread = call(
            lambda *refs: local_kernel(plan, along, *refs),
            [
                ends, inner, carry1, vertical, kernel, send_a, send_b, recv_a, recv_b, const(plan.even),
                const(plan.odd), const(plan.from_first), const(plan.from_last),
            ],
            [((width, size), F32), ((along * plan.cells3, 2 * plan.block), BF16)],
            name="local",
            cost=pl.CostEstimate(flops=4 * width * width * size, bytes_accessed=8 * 1024 * 1024, transcendentals=0),
        )
        (out,) = call(
            lambda *refs: last_kernel(plan, along, *refs),
            [right, *arrived, vertical, spread, const(plan.final), base],
            [((width, rows, cols), BF16)],
            [
                VMEM((parts, width * HALF, cols), F32),
                VMEM((parts, width, HALF, cols), BF16),
                pltpu.SemaphoreType.DMA((parts,)),
            ],
            any_out=(0,),
            name="last",
        )
        return out

    spec = P(None, "gx", "gy")
    return jax.shard_map(on_device, mesh=mesh, in_specs=(spec, P(), P()), out_specs=spec, check_vma=False)
```

```python
import jax
import jax.numpy as jnp
import ml_dtypes
import numpy as np
from jax import lax
from jax.experimental import pallas as pl
from jax.experimental.pallas import tpu as pltpu
from jax.sharding import PartitionSpec as P

BF16 = jnp.bfloat16
F32 = jnp.float32
PART = 8
VMEM = pltpu.VMEM


def hat(level, fine, cell):
    size = 2**level
    return np.maximum(0.0, 1.0 - np.abs(fine - size * cell) / size)


def weights(level, xs, ys, cell_x, cell_y):
    wx = hat(level, np.asarray(xs)[:, None], np.asarray(cell_x)[None, :])
    wy = hat(level, np.asarray(ys)[:, None], np.asarray(cell_y)[None, :])
    return (wx[:, None, :] * wy[None, :, :]).reshape(len(xs) * len(ys), len(cell_x))


def up16(n):
    return -(-n // 16) * 16


class Plan:
    def __init__(self, rows, cols):
        self.rows, self.cols = rows, cols
        ys = range(cols)
        counts = [(rows >> k, cols >> k) for k in range(4)]
        self.counts = counts
        row_cells = [(k, c) for k in (1, 2, 3) for c in range(counts[k][1] + 1)]
        self.row_cells = row_cells
        self.row_size = up16(len(row_cells))
        assert self.row_size == 128
        n3, m3 = counts[3][0] + 1, counts[3][1] + 1
        self.cells3 = up16(n3 * m3)
        self.block = -(-n3 * m3 // 128) * 128
        self.edge = (n3 * m3) // 16 * 16
        self.spare = n3 * m3 - self.edge
        level3 = [(3, r, c) for r in range(n3) for c in range(m3)]
        edge = [(k, r) for k in (1, 2) for r in range(counts[k][0] + 1)]
        self.message = up16(len(level3) + len(edge))
        self.edge_size = self.message - self.edge
        cells = []
        for side in (1, 0):
            part = [(k, r, side * counts[k][1]) for k, r in edge]
            part = (level3[self.edge :] if side else [None] * self.spare) + part
            cells += (level3[: self.edge] if side else []) + part + [None] * (self.edge_size - len(part))
        cells += [None] * (-len(cells) % 16)
        self.cells = len(cells)

        def table(cells, xs):
            out = np.zeros((len(cells), len(xs) * cols))
            for k in (1, 2, 3):
                where = [i for i, cell in enumerate(cells) if cell is not None and cell[0] == k]
                at = [cells[i] for i in where]
                out[where] = weights(k, xs, ys, [c[1] for c in at], [c[2] for c in at]).T
            return out

        self.cell_list = cells
        merge = np.zeros((len(cells), 2 * self.row_size))
        for i, cell in enumerate(cells):
            if cell is None:
                continue
            k, r, c = cell
            if r == 0:
                merge[i, row_cells.index((k, c))] = 1
            if r == counts[k][0]:
                merge[i, self.row_size + row_cells.index((k, c))] = 1
        self.merge = merge
        c1 = counts[1][1]
        grid = lambda n, m: (np.repeat(np.arange(n), m), np.tile(np.arange(m), n))
        self.even = weights(1, range(0, 2), ys, *grid(2, c1)).T
        self.odd = weights(1, range(2, 4), ys, *grid(4, c1)).T
        def from_row(xs, ends):
            out = np.zeros((2 * self.row_size, 4 * cols))
            for i, (k, c) in enumerate(row_cells):
                if k < 3 and c < counts[k][1]:
                    out[(k - 1) * self.row_size + i] = weights(k, xs, ys, [ends[k]], [c])[:, 0]
            return out

        self.from_first = from_row(range(0, 4), (0, 0, 0))
        self.from_last = from_row(range(rows - 4, rows), [n for n, _ in counts])
        final = [c for c in level3] + [None] * (self.block - len(level3))
        for k in (1, 2):
            for side in (0, 1):
                part = [None] * self.spare
                for level, r in edge:
                    part.append((k, r, side * counts[k][1]) if level == k else None)
                final += part + [None] * (self.edge_size - len(part))
        self.final_size = len(final)
        self.final = table(final, range(rows))


def const(table):
    return jnp.asarray(np.asarray(table).astype(ml_dtypes.bfloat16))


def dot(a, b):
    return jnp.dot(a, b, preferred_element_type=F32)


def dot_nt(a, b):
    return lax.dot_general(a, b, (((1,), (1,)), ((), ())), preferred_element_type=F32)


def ramp(size, offset):
    return jnp.maximum(0, size - jnp.abs(offset))


def cell_tables(cells, shape):
    index = lax.broadcasted_iota(jnp.int32, shape, 0)
    width, first, second = index * 0, index * 0, index * 0
    at = 0
    while at < len(cells):
        if cells[at] is None:
            at += 1
            continue
        k, r, c = cells[at]
        stop = at + 1
        step = None
        while stop < len(cells) and cells[stop] is not None and cells[stop][0] == k:
            move = (cells[stop][1] - cells[stop - 1][1], cells[stop][2] - cells[stop - 1][2])
            if step is None and move in ((0, 1), (1, 0)):
                step = move
            if move != step:
                break
            stop += 1
        step = step or (0, 0)
        mine = (index >= at) & (index < stop)
        width = jnp.where(mine, 2**k, width)
        first = jnp.where(mine, r + step[0] * (index - at), first)
        second = jnp.where(mine, c + step[1] * (index - at), second)
        at = stop
    return width, first, second


def split(index, size, count):
    high = index * 0
    for i in range(1, count):
        high = high + jnp.where(index >= i * size, 1, 0)
    return high, index - high * size


def first_kernel(plan, x_ref, v_in_ref, raw_ref, ends_ref, a_ref, b_ref, v_ref, column_ref, t1_ref, t2_ref, nat, sem):
    rows, cols = plan.rows, plan.cols
    width = x_ref.shape[0]
    last = rows // PART - 1
    copies = [
        pltpu.make_async_copy(x_ref.at[:, pl.ds(h * PART, PART), :], raw_ref.at[h], sem.at[h]) for h in range(last + 1)
    ]
    order = [copies[0], copies[last], *copies[1:last], pltpu.make_async_copy(v_in_ref, v_ref, sem.at[last + 1])]
    for copy in order:
        copy.start()
    even = lax.rem(lax.axis_index("gx"), 2) == 0

    shape = (plan.cells, cols)
    size, first, second = cell_tables(plan.cell_list, shape)
    y = lax.broadcasted_iota(jnp.int32, shape, 1)
    inverse = jnp.where(size == 2, 0.25, jnp.where(size == 4, 0.0625, 0.015625))
    along = ramp(size, y - size * second).astype(F32) * inverse
    size, start = size.astype(F32), (size * first).astype(F32)
    for x in range(rows):
        column_ref[:, pl.ds(x * cols, cols)] = (ramp(size, start - x) * along).astype(BF16)
    n1, c1 = plan.counts[1]
    n2, c2 = plan.counts[2]
    shape = (cols, 4 * c1)
    i, c = split(lax.broadcasted_iota(jnp.int32, shape, 1), c1, 4)
    along = ramp(2, lax.broadcasted_iota(jnp.int32, shape, 0) - 2 * c).astype(F32) * 0.25
    i = 2 * i[:1]
    for x in range(9):
        t1_ref[pl.ds(x * cols, cols), :] = (ramp(2, i - (x - 1)).astype(F32) * along).astype(BF16)
    shape = (c1, n2 * c2)
    i, c = split(lax.broadcasted_iota(jnp.int32, shape, 1), c2, n2)
    along = ramp(2, lax.broadcasted_iota(jnp.int32, shape, 0) - 2 * c).astype(F32) * 0.25
    i = 2 * i[:1]
    for x in range(n1):
        t2_ref[pl.ds(x * c1, c1), :] = (ramp(2, i - x).astype(F32) * along).astype(BF16)
    shape = (plan.row_size, cols)
    cells = [(k, 0, c) for k, c in plan.row_cells]
    size, _, second = cell_tables(cells, shape)
    y = lax.broadcasted_iota(jnp.int32, shape, 1)
    inverse = jnp.where(size == 2, 0.25, jnp.where(size == 4, 0.0625, 0.015625))
    along = ramp(size, y - size * second).astype(F32) * inverse
    size = size.astype(F32)

    def message(h, place, end):
        copies[h].wait()
        nat[place] = raw_ref[h].astype(F32).reshape(width * PART, cols)
        for x in range(PART):
            row = nat[place, pl.ds(x, width, stride=PART), :]
            ends_ref[:, pl.ds((place * PART + x) * cols, cols)] = row.astype(BF16)
        total = None
        for x in range(0, PART, 2):
            table = [(ramp(size, size * 0 + (end - x - i)) * along).astype(BF16) for i in range(2)]
            term = dot_nt(jnp.concatenate(table, axis=1), ends_ref[:, pl.ds((place * PART + x) * cols, 2 * cols)])
            total = term if total is None else total + term
        return total.astype(BF16)

    low = message(0, 0, 0)
    up = message(last, 1, PART)
    a_ref[...] = jnp.where(even, up, low)
    b_ref[...] = jnp.where(even, low, up)
    for copy in order[2:]:
        copy.wait()


class Rows:
    def __init__(self, plan, ends_ref, inner_ref):
        self.plan, self.ends, self.inner = plan, ends_ref, inner_ref

    def __call__(self, x, count):
        rows, cols = self.plan.rows, self.plan.cols
        if x < 8:
            return self.ends[:, pl.ds(x * cols, count * cols)]
        if x >= rows - 8:
            return self.ends[:, pl.ds((x - rows + 16) * cols, count * cols)]
        return self.inner[:, pl.ds((x - 8) * cols, count * cols)]


def inner_kernel(
    plan, raw_ref, ends_ref, v_ref, column_ref, t1_ref, t2_ref, inner_ref, own_ref, carry1_ref, nat, level1
):
    rows, cols = plan.rows, plan.cols
    width = ends_ref.shape[0]
    for h in range(1, rows // PART - 1):
        nat[h - 1] = raw_ref[h].astype(F32).reshape(width * PART, cols)
        for x in range(PART):
            row = nat[h - 1, pl.ds(x, width, stride=PART), :]
            inner_ref[:, pl.ds(((h - 1) * PART + x) * cols, cols)] = row.astype(BF16)
    fine = Rows(plan, ends_ref, inner_ref)
    total = None
    for x in range(0, rows, 2):
        term = dot_nt(column_ref[:, pl.ds(x * cols, 2 * cols)], fine(x, 2))
        total = term if total is None else total + term
    own_ref[...] = total
    n1, c1 = plan.counts[1]
    for k in range(rows // 8):
        total = None
        for j in range(4):
            term = dot(fine(8 * k + 2 * j, 2), t1_ref[pl.ds((2 * j + 1) * cols, 2 * cols), :])
            total = term if total is None else total + term
        if k > 0:
            total = total + dot(fine(8 * k - 1, 1), t1_ref[pl.ds(0, cols), :])
        level1[:, pl.ds(4 * k * c1, 4 * c1)] = (total * (1 / 1.5)).astype(BF16)
    level2 = (dot(level1[...], t2_ref[...]) * (1 / 1.5)).astype(BF16)
    mixed2 = (dot(v_ref[2], level2) * (1 / 1.5)).astype(BF16)
    step = 4 * c1
    for k in range(n1 * c1 // step):
        lanes = pl.ds(k * step, step)
        mixed1 = dot(v_ref[1], level1[:, lanes]) + dot_nt(mixed2, t2_ref[lanes, :])
        carry1_ref[:, lanes] = (mixed1 * (1 / 1.5)).astype(BF16)


def merge_kernel(plan, own_ref, a_ref, b_ref, merge_ref, right_ref, left_ref, block_ref):
    even = lax.rem(lax.axis_index("gx"), 2) == 0
    size = plan.row_size
    a, b = a_ref[...], b_ref[...]
    before, after = jnp.where(even, b, a), jnp.where(even, a, b)
    total32 = own_ref[...] + dot(merge_ref[:, :size], before) + dot(merge_ref[:, size:], after)
    total = total32.astype(BF16)
    right_ref[...] = total[: plan.message]
    left_ref[: plan.edge] = total[: plan.edge]
    row = lax.broadcasted_iota(jnp.int32, (plan.edge_size, total.shape[1]), 0)
    tile = jnp.where(row < plan.spare, total32[plan.edge : plan.message], total32[plan.message :])
    left_ref[plan.edge :] = tile.astype(BF16)
    block_ref[...] = total[: plan.cells3]


def local_kernel(
    plan, count, ends_ref, inner_ref, carry1, v_ref, k_ref, sa_ref, sb_ref, ra_ref, rb_ref, even_ref, odd_ref,
    first_ref, last_ref, base_ref, spread_ref,
):
    rows, cols = plan.rows, plan.cols
    n1, c1 = plan.counts[1]
    fine = Rows(plan, ends_ref, inner_ref)

    even = lax.rem(lax.axis_index("gx"), 2) == 0
    a, b = ra_ref[...], rb_ref[...]
    before, after = jnp.where(even, b, a), jnp.where(even, a, b)
    own = jnp.where(even, sa_ref[...], sb_ref[...])
    after = (after.astype(F32) + own.astype(F32)).astype(BF16)

    def mixed_rows(message):
        one = dot_nt(v_ref[1], message) * (1 / 1.5**2)
        two = dot_nt(v_ref[2], message) * (1 / 1.5**4)
        return jnp.concatenate([one, two], axis=1).astype(BF16)

    first, last = mixed_rows(before), mixed_rows(after)
    pairs = rows // 2
    for i in range(pairs):
        lanes = pl.ds(2 * i * cols, 2 * cols)
        total = dot(v_ref[0], fine(2 * i, 2))
        if i % 2 == 0:
            total = total + dot(carry1[:, pl.ds(i * c1, 2 * c1)], even_ref[...])
        elif i < pairs - 1:
            total = total + dot(carry1[:, pl.ds((i - 1) * c1, 4 * c1)], odd_ref[...])
        else:
            total = total + dot(carry1[:, pl.ds((i - 1) * c1, 2 * c1)], odd_ref[pl.ds(0, 2 * c1), :])
        if i < 2:
            total = total + dot(first, first_ref[:, pl.ds(2 * i * cols, 2 * cols)])
        if i >= pairs - 2:
            total = total + dot(last, last_ref[:, pl.ds(2 * (i - pairs + 2) * cols, 2 * cols)])
        base_ref[:, lanes] = total

    n3, m3 = plan.counts[3][0] + 1, plan.counts[3][1] + 1
    size = k_ref.shape[0]
    block, cells3 = plan.block, plan.cells3
    z = lax.axis_index("gy")

    def parts(shape, dim):
        index = lax.broadcasted_iota(jnp.int32, shape, dim)
        row = jnp.zeros(shape, jnp.int32)
        for r in range(1, n3 + 1):
            row = row + jnp.where(index >= r * m3, 1, 0)
        return row, index - row * m3

    def one(mask):
        return jnp.where(mask, 1.0, 0.0).astype(BF16)

    row, col = parts((size, block), 1)
    place = lax.broadcasted_iota(jnp.int32, (size, block), 0)
    picked = dot(k_ref[...], one((place == z * (m3 - 1) + col) & (row < n3))).astype(BF16)
    source_row, source_col = parts((cells3, block), 0)
    target_row, target_col = parts((cells3, block), 1)
    same = (target_row == source_row) & (target_row < n3)
    target = z * (m3 - 1) + target_col
    _, col = parts((cells3, size), 0)
    place = lax.broadcasted_iota(jnp.int32, (cells3, size), 1)
    for d in range(count):
        start = lax.rem(z - d + count, count) * (m3 - 1)
        spread = jnp.where(same, dot(one(place == start + col), picked), 0.0).astype(BF16)
        keep = one(same & (target == start + source_col) & (target < size))
        spread_ref[pl.ds(d * cells3, cells3), :block] = spread
        spread_ref[pl.ds(d * cells3, cells3), block:] = keep


def last_kernel(plan, count, *refs):
    own_ref, *in_refs = refs[:count]
    v_ref, spread_ref, final_ref, base_ref, out_ref, nat, buf, sem = refs[count:]
    rows, cols = plan.rows, plan.cols
    width = v_ref.shape[1]
    block = plan.block
    z = lax.axis_index("gy")
    level3 = jnp.concatenate([own_ref[: plan.cells3]] + [ref[: plan.cells3] for ref in in_refs], axis=0)
    mixed = (dot_nt(v_ref[3], level3) * (1 / 1.5**3)).astype(BF16)
    carry = dot(mixed, spread_ref[...])
    carry = (carry[:, :block] + carry[:, block:]) * (1 / 1.5**3)
    left = in_refs[0][plan.edge :]
    right = (in_refs[-1][plan.edge :].astype(F32) + own_ref[plan.edge :].astype(F32)).astype(BF16)
    left = jnp.where(z > 0, left, jnp.zeros_like(left))
    right = jnp.where(z < count - 1, right, jnp.zeros_like(right))
    edges = jnp.concatenate([left, right], axis=0)
    one = dot_nt(v_ref[1], edges) * (1 / 1.5**2)
    two = dot_nt(v_ref[2], edges) * (1 / 1.5**4)
    parts = jnp.concatenate([carry, one, two], axis=1).astype(BF16)
    copies = []
    for h in range(rows // PART):
        for x in range(0, PART, 2):
            lanes = pl.ds((h * PART + x) * cols, 2 * cols)
            total = base_ref[:, lanes] + dot(parts, final_ref[:, lanes])
            nat[h, pl.ds(x, width, stride=PART), :] = total[:, :cols]
            nat[h, pl.ds(x + 1, width, stride=PART), :] = total[:, cols:]
        buf[h] = nat[h].reshape(width, PART, cols).astype(BF16)
        copy = pltpu.make_async_copy(buf.at[h], out_ref.at[:, pl.ds(h * PART, PART), :], sem.at[h])
        copy.start()
        copies.append(copy)
    for copy in copies:
        copy.wait()


LIMIT = 14 * 1024 * 1024


def call(kernel, ins, outs, scratch=(), hbm=(), any_out=(), name=None, cost=None):
    specs = [pl.BlockSpec(memory_space=pl.ANY if i in hbm else VMEM) for i in range(len(ins))]
    out_specs = [pl.BlockSpec(memory_space=pl.ANY if i in any_out else VMEM) for i in range(len(outs))]
    out_shape = [
        jax.ShapeDtypeStruct(s, t) if i in any_out else VMEM(s, t) for i, (s, t) in enumerate(outs)
    ]
    ins = [pltpu.with_memory_space_constraint(x, pltpu.HBM if i in hbm else VMEM) for i, x in enumerate(ins)]
    return pl.pallas_call(
        kernel,
        in_specs=specs,
        out_specs=out_specs,
        out_shape=out_shape,
        scratch_shapes=list(scratch),
        compiler_params=pltpu.CompilerParams(vmem_limit_bytes=LIMIT),
        cost_estimate=cost,
        name=name,
    )(*ins)


def solution(mesh):
    across, along = mesh.shape["gx"], mesh.shape["gy"]

    def swap(x, first):
        def partner(i):
            return i ^ 1 if first else (i + 1 if i % 2 else i - 1) % across

        return lax.ppermute(x, "gx", [(i, partner(i)) for i in range(across)])

    def on_device(gradient, vertical, kernel):
        width, rows, cols = gradient.shape
        plan = Plan(rows, cols)
        parts = rows // PART
        n1, c1 = plan.counts[1]
        n2, c2 = plan.counts[2]
        size = rows * cols
        row_message = ((plan.row_size, width), BF16)
        cells = plan.cells
        raw, ends, send_a, send_b, vertical, column, to_level1, to_level2 = call(
            lambda *refs: first_kernel(plan, *refs),
            [gradient, vertical],
            [
                ((parts, width, PART, cols), BF16), ((width, 2 * PART * cols), BF16), row_message, row_message,
                (vertical.shape, BF16), ((cells, size), BF16), ((9 * cols, 4 * c1), BF16), ((n1 * c1, n2 * c2), BF16),
            ],
            [VMEM((2, width * PART, cols), F32), pltpu.SemaphoreType.DMA((parts + 1,))],
            hbm=(0, 1),
            name="first",
        )
        recv_b = swap(send_b, False)
        recv_a = swap(send_a, True)
        inner, own, carry1 = call(
            lambda *refs: inner_kernel(plan, *refs),
            [
                raw, ends, vertical, column, to_level1, to_level2,
            ],
            [((width, size - 16 * cols), BF16), ((cells, width), F32), ((width, size // 4), BF16)],
            [VMEM((parts - 2, width * PART, cols), F32), VMEM((width, size // 4), BF16)],
            name="inner",
            cost=pl.CostEstimate(flops=3 * cells * width * size, bytes_accessed=4 * 1024 * 1024, transcendentals=0),
        )
        right, left, block = call(
            lambda *refs: merge_kernel(plan, *refs),
            [own, recv_a, recv_b, const(plan.merge)],
            [((plan.message, width), BF16), ((plan.message, width), BF16), ((plan.cells3, width), BF16)],
            name="merge",
        )
        messages = [block] * (along + 1)
        messages[1], messages[along - 1] = right, left
        arrived = [
            lax.ppermute(messages[d], "gy", [(i, (i + d) % along) for i in range(along)]) for d in range(1, along)
        ]
        base, spread = call(
            lambda *refs: local_kernel(plan, along, *refs),
            [
                ends, inner, carry1, vertical, kernel, send_a, send_b, recv_a, recv_b, const(plan.even),
                const(plan.odd), const(plan.from_first), const(plan.from_last),
            ],
            [((width, size), F32), ((along * plan.cells3, 2 * plan.block), BF16)],
            name="local",
            cost=pl.CostEstimate(flops=4 * width * width * size, bytes_accessed=8 * 1024 * 1024, transcendentals=0),
        )
        (out,) = call(
            lambda *refs: last_kernel(plan, along, *refs),
            [right, *arrived, vertical, spread, const(plan.final), base],
            [((width, rows, cols), BF16)],
            [
                VMEM((parts, width * PART, cols), F32),
                VMEM((parts, width, PART, cols), BF16),
                pltpu.SemaphoreType.DMA((parts,)),
            ],
            any_out=(0,),
            name="last",
        )
        return out

    spec = P(None, "gx", "gy")
    return jax.shard_map(on_device, mesh=mesh, in_specs=(spec, P(), P()), out_specs=spec, check_vma=False)
```

```python
import jax
import jax.numpy as jnp
import ml_dtypes
import numpy as np
from jax import lax
from jax.experimental import pallas as pl
from jax.experimental.pallas import tpu as pltpu
from jax.sharding import PartitionSpec as P

BF16 = jnp.bfloat16
F32 = jnp.float32
PART = 8
CHUNKS = 2
VMEM = pltpu.VMEM


def hat(level, fine, cell):
    size = 2**level
    return np.maximum(0.0, 1.0 - np.abs(fine - size * cell) / size)


def weights(level, xs, ys, cell_x, cell_y):
    wx = hat(level, np.asarray(xs)[:, None], np.asarray(cell_x)[None, :])
    wy = hat(level, np.asarray(ys)[:, None], np.asarray(cell_y)[None, :])
    return (wx[:, None, :] * wy[None, :, :]).reshape(len(xs) * len(ys), len(cell_x))


def routes(count):
    if count == 4:
        return [(1, 3, 0, 2), (3, 2, 1, 0), (2, 0, 3, 1)]
    return [[(i + d) % count for i in range(count)] for d in range(1, count)]


def arrivals(count):
    return [
        [(k, step.index(z)) for k, step in enumerate(routes(count)) if step[z] != z] for z in range(count)
    ]


def chosen(index, values):
    result = index * 0
    for i, value in enumerate(values):
        result = result + jnp.where(index == i, value, 0)
    return result


def up16(n):
    return -(-n // 16) * 16


class Plan:
    def __init__(self, rows, cols):
        self.rows, self.cols = rows, cols
        ys = range(cols)
        counts = [(rows >> k, cols >> k) for k in range(4)]
        self.counts = counts
        row_cells = [(k, c) for k in (1, 2, 3) for c in range(counts[k][1] + 1)]
        self.row_cells = row_cells
        self.row_size = up16(len(row_cells))
        assert self.row_size == 128
        n3, m3 = counts[3][0] + 1, counts[3][1] + 1
        self.cells3 = up16(n3 * m3)
        self.block = -(-n3 * m3 // 128) * 128
        self.edge = (n3 * m3) // 16 * 16
        self.spare = n3 * m3 - self.edge
        level3 = [(3, r, c) for r in range(n3) for c in range(m3)]
        edge = [(k, r) for k in (1, 2) for r in range(counts[k][0] + 1)]
        self.message = up16(len(level3) + len(edge))
        self.edge_size = self.message - self.edge
        cells = []
        for side in (1, 0):
            part = [(k, r, side * counts[k][1]) for k, r in edge]
            part = (level3[self.edge :] if side else [None] * self.spare) + part
            cells += (level3[: self.edge] if side else []) + part + [None] * (self.edge_size - len(part))
        cells += [None] * (-len(cells) % 16)
        self.cells = len(cells)

        def table(cells, xs):
            out = np.zeros((len(cells), len(xs) * cols))
            for k in (1, 2, 3):
                where = [i for i, cell in enumerate(cells) if cell is not None and cell[0] == k]
                at = [cells[i] for i in where]
                out[where] = weights(k, xs, ys, [c[1] for c in at], [c[2] for c in at]).T
            return out

        self.cell_list = cells
        merge = np.zeros((len(cells), 2 * self.row_size))
        for i, cell in enumerate(cells):
            if cell is None:
                continue
            k, r, c = cell
            if r == 0:
                merge[i, row_cells.index((k, c))] = 1
            if r == counts[k][0]:
                merge[i, self.row_size + row_cells.index((k, c))] = 1
        self.merge = merge
        c1 = counts[1][1]
        grid = lambda n, m: (np.repeat(np.arange(n), m), np.tile(np.arange(m), n))
        self.even = weights(1, range(0, 2), ys, *grid(2, c1)).T
        self.odd = weights(1, range(2, 4), ys, *grid(4, c1)).T
        def from_row(xs, ends):
            out = np.zeros((2 * self.row_size, 4 * cols))
            for i, (k, c) in enumerate(row_cells):
                if k < 3 and c < counts[k][1]:
                    out[(k - 1) * self.row_size + i] = weights(k, xs, ys, [ends[k]], [c])[:, 0]
            return out

        self.from_first = from_row(range(0, 4), (0, 0, 0))
        self.from_last = from_row(range(rows - 4, rows), [n for n, _ in counts])
        final = [c for c in level3] + [None] * (self.block - len(level3))
        for k in (1, 2):
            for side in (0, 1):
                part = [None] * self.spare
                for level, r in edge:
                    part.append((k, r, side * counts[k][1]) if level == k else None)
                final += part + [None] * (self.edge_size - len(part))
        self.final_size = len(final)
        self.final = table(final, range(rows))


def const(table):
    return jnp.asarray(np.asarray(table).astype(ml_dtypes.bfloat16))


def dot(a, b):
    return jnp.dot(a, b, preferred_element_type=F32)


def dot_nt(a, b):
    return lax.dot_general(a, b, (((1,), (1,)), ((), ())), preferred_element_type=F32)


def ramp(size, offset):
    return jnp.maximum(0, size - jnp.abs(offset))


def cell_tables(cells, shape):
    index = lax.broadcasted_iota(jnp.int32, shape, 0)
    width, first, second = index * 0, index * 0, index * 0
    at = 0
    while at < len(cells):
        if cells[at] is None:
            at += 1
            continue
        k, r, c = cells[at]
        stop = at + 1
        step = None
        while stop < len(cells) and cells[stop] is not None and cells[stop][0] == k:
            move = (cells[stop][1] - cells[stop - 1][1], cells[stop][2] - cells[stop - 1][2])
            if step is None and move in ((0, 1), (1, 0)):
                step = move
            if move != step:
                break
            stop += 1
        step = step or (0, 0)
        mine = (index >= at) & (index < stop)
        width = jnp.where(mine, 2**k, width)
        first = jnp.where(mine, r + step[0] * (index - at), first)
        second = jnp.where(mine, c + step[1] * (index - at), second)
        at = stop
    return width, first, second


def split(index, size, count):
    high = index * 0
    for i in range(1, count):
        high = high + jnp.where(index >= i * size, 1, 0)
    return high, index - high * size


def first_kernel(plan, x_ref, raw_ref, ends_ref, a_ref, b_ref, column_ref, t1_ref, t2_ref, nat, sem):
    rows, cols = plan.rows, plan.cols
    width = x_ref.shape[0]
    last = rows // PART - 1
    chunk = width // CHUNKS

    def fetch(h, start, count, i):
        fields = pl.ds(start, count)
        return pltpu.make_async_copy(x_ref.at[fields, pl.ds(h * PART, PART), :], raw_ref.at[h, fields], sem.at[i])

    copies = [
        [fetch(h, c * chunk, chunk, 2 * c + place) for place, h in enumerate((0, last))] for c in range(CHUNKS)
    ]
    copies.append([fetch(h, 0, width, 2 * CHUNKS + h - 1) for h in range(1, last)])
    for group in copies:
        for copy in group:
            copy.start()
    even = lax.rem(lax.axis_index("gx"), 2) == 0

    shape = (plan.cells, cols)
    size, first, second = cell_tables(plan.cell_list, shape)
    y = lax.broadcasted_iota(jnp.int32, shape, 1)
    inverse = jnp.where(size == 2, 0.25, jnp.where(size == 4, 0.0625, 0.015625))
    along = ramp(size, y - size * second).astype(F32) * inverse
    size, start = size.astype(F32), (size * first).astype(F32)
    for x in range(rows):
        column_ref[:, pl.ds(x * cols, cols)] = (ramp(size, start - x) * along).astype(BF16)
    n1, c1 = plan.counts[1]
    n2, c2 = plan.counts[2]
    shape = (cols, 4 * c1)
    i, c = split(lax.broadcasted_iota(jnp.int32, shape, 1), c1, 4)
    along = ramp(2, lax.broadcasted_iota(jnp.int32, shape, 0) - 2 * c).astype(F32) * 0.25
    i = 2 * i[:1]
    for x in range(9):
        t1_ref[pl.ds(x * cols, cols), :] = (ramp(2, i - (x - 1)).astype(F32) * along).astype(BF16)
    shape = (c1, n2 * c2)
    i, c = split(lax.broadcasted_iota(jnp.int32, shape, 1), c2, n2)
    along = ramp(2, lax.broadcasted_iota(jnp.int32, shape, 0) - 2 * c).astype(F32) * 0.25
    i = 2 * i[:1]
    for x in range(n1):
        t2_ref[pl.ds(x * c1, c1), :] = (ramp(2, i - x).astype(F32) * along).astype(BF16)
    shape = (plan.row_size, cols)
    cells = [(k, 0, c) for k, c in plan.row_cells]
    size, _, second = cell_tables(cells, shape)
    y = lax.broadcasted_iota(jnp.int32, shape, 1)
    inverse = jnp.where(size == 2, 0.25, jnp.where(size == 4, 0.0625, 0.015625))
    along = ramp(size, y - size * second).astype(F32) * inverse
    size = size.astype(F32)

    def message(place, end):
        total = None
        for x in range(0, PART, 2):
            table = [(ramp(size, size * 0 + (end - x - i)) * along).astype(BF16) for i in range(2)]
            term = dot_nt(jnp.concatenate(table, axis=1), ends_ref[:, pl.ds((place * PART + x) * cols, 2 * cols)])
            total = term if total is None else total + term
        return total.astype(BF16)

    for c in range(CHUNKS):
        fields = pl.ds(c * chunk, chunk)
        for place, h in enumerate((0, last)):
            copies[c][place].wait()
            nat[c, place] = raw_ref[h, fields].astype(F32).reshape(chunk * PART, cols)
            for x in range(PART):
                row = nat[c, place, pl.ds(x, chunk, stride=PART), :]
                ends_ref[fields, pl.ds((place * PART + x) * cols, cols)] = row.astype(BF16)
    low, up = message(0, 0), message(1, PART)
    a_ref[...] = jnp.where(even, up, low)
    b_ref[...] = jnp.where(even, low, up)
    for copy in copies[-1]:
        copy.wait()


class Rows:
    def __init__(self, plan, ends_ref, inner_ref):
        self.plan, self.ends, self.inner = plan, ends_ref, inner_ref

    def __call__(self, x, count):
        rows, cols = self.plan.rows, self.plan.cols
        if x < 8:
            return self.ends[:, pl.ds(x * cols, count * cols)]
        if x >= rows - 8:
            return self.ends[:, pl.ds((x - rows + 16) * cols, count * cols)]
        return self.inner[:, pl.ds((x - 8) * cols, count * cols)]


def inner_kernel(
    plan, raw_ref, ends_ref, column_ref, t1_ref, t2_ref, inner_ref, own_ref, level1, level2, nat
):
    rows, cols = plan.rows, plan.cols
    width = ends_ref.shape[0]
    for h in range(1, rows // PART - 1):
        nat[h - 1] = raw_ref[h].astype(F32).reshape(width * PART, cols)
        for x in range(PART):
            row = nat[h - 1, pl.ds(x, width, stride=PART), :]
            inner_ref[:, pl.ds(((h - 1) * PART + x) * cols, cols)] = row.astype(BF16)
    fine = Rows(plan, ends_ref, inner_ref)
    total = None
    for x in range(0, rows, 2):
        term = dot_nt(column_ref[:, pl.ds(x * cols, 2 * cols)], fine(x, 2))
        total = term if total is None else total + term
    own_ref[...] = total
    n1, c1 = plan.counts[1]
    for k in range(rows // 8):
        total = None
        for j in range(4):
            term = dot(fine(8 * k + 2 * j, 2), t1_ref[pl.ds((2 * j + 1) * cols, 2 * cols), :])
            total = term if total is None else total + term
        if k > 0:
            total = total + dot(fine(8 * k - 1, 1), t1_ref[pl.ds(0, cols), :])
        level1[:, pl.ds(4 * k * c1, 4 * c1)] = (total * (1 / 1.5)).astype(BF16)
    level2[...] = (dot(level1[...], t2_ref[...]) * (1 / 1.5)).astype(BF16)


def merge_kernel(plan, count, own_ref, b_ref, a_ref, merge_ref, right_ref, *out_refs):
    even = lax.rem(lax.axis_index("gx"), 2) == 0
    size = plan.row_size
    a, b = a_ref[...], b_ref[...]
    before, after = jnp.where(even, b, a), jnp.where(even, a, b)
    total32 = own_ref[...] + dot(merge_ref[:, :size], before) + dot(merge_ref[:, size:], after)
    total = total32.astype(BF16)
    right_ref[...] = total[: plan.message]
    row = lax.broadcasted_iota(jnp.int32, (plan.edge_size, total.shape[1]), 0)
    tile = jnp.where(row < plan.spare, total32[plan.edge : plan.message], total32[plan.message :])
    right, left = total[plan.edge : plan.message], tile.astype(BF16)
    z = lax.axis_index("gy")
    for step, ref in zip(routes(count), out_refs):
        to_left = chosen(z, [int(step[i] == i - 1) for i in range(count)]) == 1
        ref[: plan.edge] = total[: plan.edge]
        ref[plan.edge :] = jnp.where(to_left, left, right)


def source_of(z, count, d):
    return z if d == 0 else chosen(z, [got[d - 1][1] for got in arrivals(count)])


def local_kernel(
    plan, count, ends_ref, inner_ref, level1, level2, t2_ref, v_ref, k_ref, sa_ref, sb_ref, ra_ref, rb_ref, even_ref, odd_ref,
    first_ref, last_ref, base_ref, spread_ref, carry1,
):
    rows, cols = plan.rows, plan.cols
    n1, c1 = plan.counts[1]
    fine = Rows(plan, ends_ref, inner_ref)
    mixed2 = (dot(v_ref[2], level2[...]) * (1 / 1.5)).astype(BF16)
    step = 4 * c1
    for k in range(n1 * c1 // step):
        lanes = pl.ds(k * step, step)
        mixed1 = dot(v_ref[1], level1[:, lanes]) + dot_nt(mixed2, t2_ref[lanes, :])
        carry1[:, lanes] = (mixed1 * (1 / 1.5)).astype(BF16)

    even = lax.rem(lax.axis_index("gx"), 2) == 0
    a, b = ra_ref[...], rb_ref[...]
    before, after = jnp.where(even, b, a), jnp.where(even, a, b)
    own = jnp.where(even, sa_ref[...], sb_ref[...])
    after = (after.astype(F32) + own.astype(F32)).astype(BF16)

    def mixed_rows(message):
        one = dot_nt(v_ref[1], message) * (1 / 1.5**2)
        two = dot_nt(v_ref[2], message) * (1 / 1.5**4)
        return jnp.concatenate([one, two], axis=1).astype(BF16)

    first, last = mixed_rows(before), mixed_rows(after)
    pairs = rows // 2
    for i in range(pairs):
        lanes = pl.ds(2 * i * cols, 2 * cols)
        total = dot(v_ref[0], fine(2 * i, 2))
        if i % 2 == 0:
            total = total + dot(carry1[:, pl.ds(i * c1, 2 * c1)], even_ref[...])
        elif i < pairs - 1:
            total = total + dot(carry1[:, pl.ds((i - 1) * c1, 4 * c1)], odd_ref[...])
        else:
            total = total + dot(carry1[:, pl.ds((i - 1) * c1, 2 * c1)], odd_ref[pl.ds(0, 2 * c1), :])
        if i < 2:
            total = total + dot(first, first_ref[:, pl.ds(2 * i * cols, 2 * cols)])
        if i >= pairs - 2:
            total = total + dot(last, last_ref[:, pl.ds(2 * (i - pairs + 2) * cols, 2 * cols)])
        base_ref[:, lanes] = total

    n3, m3 = plan.counts[3][0] + 1, plan.counts[3][1] + 1
    size = k_ref.shape[0]
    block, cells3 = plan.block, plan.cells3
    z = lax.axis_index("gy")

    def parts(shape, dim):
        index = lax.broadcasted_iota(jnp.int32, shape, dim)
        row = jnp.zeros(shape, jnp.int32)
        for r in range(1, n3 + 1):
            row = row + jnp.where(index >= r * m3, 1, 0)
        return row, index - row * m3

    def one(mask):
        return jnp.where(mask, 1.0, 0.0).astype(BF16)

    row, col = parts((size, block), 1)
    place = lax.broadcasted_iota(jnp.int32, (size, block), 0)
    picked = dot(k_ref[...], one((place == z * (m3 - 1) + col) & (row < n3))).astype(BF16)
    source_row, source_col = parts((cells3, block), 0)
    target_row, target_col = parts((cells3, block), 1)
    same = (target_row == source_row) & (target_row < n3)
    target = z * (m3 - 1) + target_col
    _, col = parts((cells3, size), 0)
    place = lax.broadcasted_iota(jnp.int32, (cells3, size), 1)
    for d in range(count):
        start = source_of(z, count, d) * (m3 - 1)
        spread = jnp.where(same, dot(one(place == start + col), picked), 0.0).astype(BF16)
        keep = one(same & (target == start + source_col) & (target < size))
        spread_ref[pl.ds(d * cells3, cells3), :block] = spread
        spread_ref[pl.ds(d * cells3, cells3), block:] = keep


def last_kernel(plan, count, *refs):
    steps = routes(count)
    own_ref, *in_refs = refs[: 1 + len(steps)]
    v_ref, spread_ref, final_ref, base_ref, out_ref, nat, buf, sem = refs[1 + len(steps) :]
    rows, cols = plan.rows, plan.cols
    width = v_ref.shape[1]
    block = plan.block
    z = lax.axis_index("gy")
    messages = [own_ref[...]]
    for d in range(1, count):
        step_of = [got[d - 1][0] for got in arrivals(count)]
        message = None
        for step in sorted(set(step_of)):
            value = in_refs[step][...]
            mine = chosen(z, [int(s == step) for s in step_of]) == 1
            message = value if message is None else jnp.where(mine, value, message)
        messages.append(message)
    level3 = jnp.concatenate([message[: plan.cells3] for message in messages], axis=0)
    mixed = (dot_nt(v_ref[3], level3) * (1 / 1.5**3)).astype(BF16)
    carry = dot(mixed, spread_ref[...])
    carry = (carry[:, :block] + carry[:, block:]) * (1 / 1.5**3)
    left = jnp.zeros((plan.edge_size, width), F32)
    right = own_ref[plan.edge :].astype(F32)
    for d in range(1, count):
        source, edge = source_of(z, count, d), messages[d][plan.edge :].astype(F32)
        left = left + jnp.where((source == z - 1) & (z > 0), edge, 0.0)
        right = right + jnp.where((source == z + 1) & (z < count - 1), edge, 0.0)
    left = left.astype(BF16)
    right = jnp.where(z < count - 1, right, 0.0).astype(BF16)
    edges = jnp.concatenate([left, right], axis=0)
    one = dot_nt(v_ref[1], edges) * (1 / 1.5**2)
    two = dot_nt(v_ref[2], edges) * (1 / 1.5**4)
    parts = jnp.concatenate([carry, one, two], axis=1).astype(BF16)
    copies = []
    for h in range(rows // PART):
        for x in range(0, PART, 2):
            lanes = pl.ds((h * PART + x) * cols, 2 * cols)
            total = base_ref[:, lanes] + dot(parts, final_ref[:, lanes])
            nat[h, pl.ds(x, width, stride=PART), :] = total[:, :cols]
            nat[h, pl.ds(x + 1, width, stride=PART), :] = total[:, cols:]
        buf[h] = nat[h].reshape(width, PART, cols).astype(BF16)
        copy = pltpu.make_async_copy(buf.at[h], out_ref.at[:, pl.ds(h * PART, PART), :], sem.at[h])
        copy.start()
        copies.append(copy)
    for copy in copies:
        copy.wait()


LIMIT = 14 * 1024 * 1024


def call(kernel, ins, outs, scratch=(), hbm=(), any_out=(), name=None, cost=None):
    specs = [pl.BlockSpec(memory_space=pl.ANY if i in hbm else VMEM) for i in range(len(ins))]
    out_specs = [pl.BlockSpec(memory_space=pl.ANY if i in any_out else VMEM) for i in range(len(outs))]
    out_shape = [
        jax.ShapeDtypeStruct(s, t) if i in any_out else VMEM(s, t) for i, (s, t) in enumerate(outs)
    ]
    ins = [pltpu.with_memory_space_constraint(x, pltpu.HBM if i in hbm else VMEM) for i, x in enumerate(ins)]
    return pl.pallas_call(
        kernel,
        in_specs=specs,
        out_specs=out_specs,
        out_shape=out_shape,
        scratch_shapes=list(scratch),
        compiler_params=pltpu.CompilerParams(vmem_limit_bytes=LIMIT),
        cost_estimate=cost,
        name=name,
    )(*ins)


def solution(mesh):
    across, along = mesh.shape["gx"], mesh.shape["gy"]

    def swap(x, first):
        def partner(i):
            return i ^ 1 if first else (i + 1 if i % 2 else i - 1) % across

        return lax.ppermute(x, "gx", [(i, partner(i)) for i in range(across)])

    def on_device(gradient, vertical, kernel):
        width, rows, cols = gradient.shape
        plan = Plan(rows, cols)
        parts = rows // PART
        n1, c1 = plan.counts[1]
        n2, c2 = plan.counts[2]
        size = rows * cols
        row_message = ((plan.row_size, width), BF16)
        cells = plan.cells
        raw, ends, send_a, send_b, column, to_level1, to_level2 = call(
            lambda *refs: first_kernel(plan, *refs),
            [gradient],
            [
                ((parts, width, PART, cols), BF16), ((width, 2 * PART * cols), BF16), row_message, row_message,
                ((cells, size), BF16), ((9 * cols, 4 * c1), BF16), ((n1 * c1, n2 * c2), BF16),
            ],
            [
                VMEM((CHUNKS, 2, width // CHUNKS * PART, cols), F32),
                pltpu.SemaphoreType.DMA((2 * CHUNKS + parts - 2,)),
            ],
            hbm=(0,),
            name="first",
        )
        recv_b = swap(send_b, False)
        recv_a = swap(send_a, True)
        inner, own, level1, level2 = call(
            lambda *refs: inner_kernel(plan, *refs),
            [raw, ends, column, to_level1, to_level2],
            [
                ((width, size - 2 * PART * cols), BF16), ((cells, width), F32), ((width, n1 * c1), BF16),
                ((width, n2 * c2), BF16),
            ],
            [VMEM((parts - 2, width * PART, cols), F32)],
            name="inner",
            cost=pl.CostEstimate(flops=3 * cells * width * size, bytes_accessed=4 * 1024 * 1024, transcendentals=0),
        )
        steps = routes(along)
        message = ((plan.message, width), BF16)
        right, *messages = call(
            lambda *refs: merge_kernel(plan, along, *refs),
            [own, recv_b, recv_a, const(plan.merge)],
            [message] * (1 + len(steps)),
            name="merge",
        )
        arrived = [lax.ppermute(x, "gy", list(enumerate(step))) for x, step in zip(messages, steps)]
        base, spread = call(
            lambda *refs: local_kernel(plan, along, *refs),
            [
                ends, inner, level1, level2, to_level2, vertical, kernel, send_a, send_b, recv_a, recv_b, const(plan.even),
                const(plan.odd), const(plan.from_first), const(plan.from_last),
            ],
            [((width, size), F32), ((along * plan.cells3, 2 * plan.block), BF16)],
            [VMEM((width, n1 * c1), BF16)],
            name="local",
            cost=pl.CostEstimate(flops=4 * width * width * size, bytes_accessed=8 * 1024 * 1024, transcendentals=0),
        )
        (out,) = call(
            lambda *refs: last_kernel(plan, along, *refs),
            [right, *arrived, vertical, spread, const(plan.final), base],
            [((width, rows, cols), BF16)],
            [
                VMEM((parts, width * PART, cols), F32),
                VMEM((parts, width, PART, cols), BF16),
                pltpu.SemaphoreType.DMA((parts,)),
            ],
            any_out=(0,),
            name="last",
        )
        return out

    spec = P(None, "gx", "gy")
    return jax.shard_map(on_device, mesh=mesh, in_specs=(spec, P(), P()), out_specs=spec, check_vma=False)
```

```python
import jax
import jax.numpy as jnp
import ml_dtypes
import numpy as np
from jax import lax
from jax.experimental import pallas as pl
from jax.experimental.pallas import tpu as pltpu
from jax.sharding import PartitionSpec as P

BF16 = jnp.bfloat16
F32 = jnp.float32
PART = 8
CHUNKS = 2
VMEM = pltpu.VMEM


def hat(level, fine, cell):
    size = 2**level
    return np.maximum(0.0, 1.0 - np.abs(fine - size * cell) / size)


def weights(level, xs, ys, cell_x, cell_y):
    wx = hat(level, np.asarray(xs)[:, None], np.asarray(cell_x)[None, :])
    wy = hat(level, np.asarray(ys)[:, None], np.asarray(cell_y)[None, :])
    return (wx[:, None, :] * wy[None, :, :]).reshape(len(xs) * len(ys), len(cell_x))


def routes(count):
    if count == 4:
        return [(1, 3, 0, 2), (3, 2, 1, 0), (2, 0, 3, 1)]
    return [[(i + d) % count for i in range(count)] for d in range(1, count)]


def arrivals(count):
    return [
        [(k, step.index(z)) for k, step in enumerate(routes(count)) if step[z] != z] for z in range(count)
    ]


def chosen(index, values):
    result = index * 0
    for i, value in enumerate(values):
        result = result + jnp.where(index == i, value, 0)
    return result


def up16(n):
    return -(-n // 16) * 16


class Plan:
    def __init__(self, rows, cols):
        self.rows, self.cols = rows, cols
        ys = range(cols)
        counts = [(rows >> k, cols >> k) for k in range(4)]
        self.counts = counts
        row_cells = [(k, c) for k in (1, 2, 3) for c in range(counts[k][1] + 1)]
        self.row_cells = row_cells
        self.row_size = up16(len(row_cells))
        assert self.row_size == 128
        n3, m3 = counts[3][0] + 1, counts[3][1] + 1
        self.cells3 = up16(n3 * m3)
        self.block = -(-n3 * m3 // 128) * 128
        self.edge = (n3 * m3) // 16 * 16
        self.spare = n3 * m3 - self.edge
        level3 = [(3, r, c) for r in range(n3) for c in range(m3)]
        edge = [(k, r) for k in (1, 2) for r in range(counts[k][0] + 1)]
        self.message = up16(len(level3) + len(edge))
        self.edge_size = self.message - self.edge
        cells = []
        for side in (1, 0):
            part = [(k, r, side * counts[k][1]) for k, r in edge]
            part = (level3[self.edge :] if side else [None] * self.spare) + part
            cells += (level3[: self.edge] if side else []) + part + [None] * (self.edge_size - len(part))
        cells += [None] * (-len(cells) % 16)
        self.cells = len(cells)

        def table(cells, xs):
            out = np.zeros((len(cells), len(xs) * cols))
            for k in (1, 2, 3):
                where = [i for i, cell in enumerate(cells) if cell is not None and cell[0] == k]
                at = [cells[i] for i in where]
                out[where] = weights(k, xs, ys, [c[1] for c in at], [c[2] for c in at]).T
            return out

        self.cell_list = cells
        merge = np.zeros((len(cells), 2 * self.row_size))
        for i, cell in enumerate(cells):
            if cell is None:
                continue
            k, r, c = cell
            if r == 0:
                merge[i, row_cells.index((k, c))] = 1
            if r == counts[k][0]:
                merge[i, self.row_size + row_cells.index((k, c))] = 1
        self.merge = merge
        c1 = counts[1][1]
        grid = lambda n, m: (np.repeat(np.arange(n), m), np.tile(np.arange(m), n))
        self.even = weights(1, range(0, 2), ys, *grid(2, c1)).T
        self.odd = weights(1, range(2, 4), ys, *grid(4, c1)).T
        def from_row(xs, ends):
            out = np.zeros((2 * self.row_size, 4 * cols))
            for i, (k, c) in enumerate(row_cells):
                if k < 3 and c < counts[k][1]:
                    out[(k - 1) * self.row_size + i] = weights(k, xs, ys, [ends[k]], [c])[:, 0]
            return out

        self.from_first = from_row(range(0, 4), (0, 0, 0))
        self.from_last = from_row(range(rows - 4, rows), [n for n, _ in counts])
        final = [c for c in level3] + [None] * (self.block - len(level3))
        for k in (1, 2):
            for side in (0, 1):
                part = [None] * self.spare
                for level, r in edge:
                    part.append((k, r, side * counts[k][1]) if level == k else None)
                final += part + [None] * (self.edge_size - len(part))
        self.final_size = len(final)
        self.final = table(final, range(rows))


def const(table):
    return jnp.asarray(np.asarray(table).astype(ml_dtypes.bfloat16))


def dot(a, b):
    return jnp.dot(a, b, preferred_element_type=F32)


def dot_nt(a, b):
    return lax.dot_general(a, b, (((1,), (1,)), ((), ())), preferred_element_type=F32)


def ramp(size, offset):
    return jnp.maximum(0, size - jnp.abs(offset))


def cell_tables(cells, shape):
    index = lax.broadcasted_iota(jnp.int32, shape, 0)
    width, first, second = index * 0, index * 0, index * 0
    at = 0
    while at < len(cells):
        if cells[at] is None:
            at += 1
            continue
        k, r, c = cells[at]
        stop = at + 1
        step = None
        while stop < len(cells) and cells[stop] is not None and cells[stop][0] == k:
            move = (cells[stop][1] - cells[stop - 1][1], cells[stop][2] - cells[stop - 1][2])
            if step is None and move in ((0, 1), (1, 0)):
                step = move
            if move != step:
                break
            stop += 1
        step = step or (0, 0)
        mine = (index >= at) & (index < stop)
        width = jnp.where(mine, 2**k, width)
        first = jnp.where(mine, r + step[0] * (index - at), first)
        second = jnp.where(mine, c + step[1] * (index - at), second)
        at = stop
    return width, first, second


def split(index, size, count):
    high = index * 0
    for i in range(1, count):
        high = high + jnp.where(index >= i * size, 1, 0)
    return high, index - high * size


def first_kernel(plan, x_ref, raw_ref, a_ref, b_ref, column_ref, t1_ref, t2_ref, nat, sums, table, sem):
    rows, cols = plan.rows, plan.cols
    width = x_ref.shape[0]
    last = rows // PART - 1
    chunk = width // CHUNKS

    def fetch(h, start, count, i):
        fields = pl.ds(start, count)
        return pltpu.make_async_copy(x_ref.at[fields, pl.ds(h * PART, PART), :], raw_ref.at[h, fields], sem.at[i])

    copies = [
        [fetch(h, c * chunk, chunk, 2 * c + place) for place, h in enumerate((0, last))] for c in range(CHUNKS)
    ]
    copies.append([fetch(h, 0, width, 2 * CHUNKS + h - 1) for h in range(1, last)])
    for group in copies:
        for copy in group:
            copy.start()
    even = lax.rem(lax.axis_index("gx"), 2) == 0

    shape = (plan.cells, cols)
    size, first, second = cell_tables(plan.cell_list, shape)
    y = lax.broadcasted_iota(jnp.int32, shape, 1)
    inverse = jnp.where(size == 2, 0.25, jnp.where(size == 4, 0.0625, 0.015625))
    along = ramp(size, y - size * second).astype(F32) * inverse
    size, start = size.astype(F32), (size * first).astype(F32)
    for x in range(rows):
        column_ref[:, pl.ds(x * cols, cols)] = (ramp(size, start - x) * along).astype(BF16)
    n1, c1 = plan.counts[1]
    n2, c2 = plan.counts[2]
    shape = (cols, 4 * c1)
    i, c = split(lax.broadcasted_iota(jnp.int32, shape, 1), c1, 4)
    along = ramp(2, lax.broadcasted_iota(jnp.int32, shape, 0) - 2 * c).astype(F32) * 0.25
    i = 2 * i[:1]
    for x in range(9):
        t1_ref[pl.ds(x * cols, cols), :] = (ramp(2, i - (x - 1)).astype(F32) * along).astype(BF16)
    shape = (c1, n2 * c2)
    i, c = split(lax.broadcasted_iota(jnp.int32, shape, 1), c2, n2)
    along = ramp(2, lax.broadcasted_iota(jnp.int32, shape, 0) - 2 * c).astype(F32) * 0.25
    i = 2 * i[:1]
    for x in range(n1):
        t2_ref[pl.ds(x * c1, c1), :] = (ramp(2, i - x).astype(F32) * along).astype(BF16)
    shape = (plan.row_size, cols)
    level, _, second = cell_tables([(k, 0, c) for k, c in plan.row_cells], shape)
    y = lax.broadcasted_iota(jnp.int32, shape, 1)
    for k in (1, 2, 3):
        weight = ramp(2**k, y - 2**k * second).astype(F32) * 0.5**k
        table[:, pl.ds((k - 1) * cols, cols)] = jnp.where(level == 2**k, weight, 0.0).astype(BF16)
    for c in range(CHUNKS):
        fields = pl.ds(c * chunk, chunk)
        for place, (h, end) in enumerate(((0, 0), (last, PART))):
            copies[c][place].wait()
            nat[c, place] = raw_ref[h, fields].astype(F32).reshape(chunk * PART, cols)
            found = [None] * 3
            for x in range(PART):
                row = nat[c, place, pl.ds(x, chunk, stride=PART), :]
                for k in range(3):
                    weight = float(hat(k + 1, x, end / 2 ** (k + 1)))
                    if weight:
                        term = row * weight
                        found[k] = term if found[k] is None else found[k] + term
            for k in range(3):
                sums[place, fields, pl.ds(k * cols, cols)] = found[k].astype(BF16)
    low, up = [dot_nt(table[...], sums[place]).astype(BF16) for place in range(2)]
    a_ref[...] = jnp.where(even, up, low)
    b_ref[...] = jnp.where(even, low, up)
    for copy in copies[-1]:
        copy.wait()


def inner_kernel(
    plan, raw_ref, column_ref, t1_ref, t2_ref, flat_ref, own_ref, level1, level2, nat
):
    rows, cols = plan.rows, plan.cols
    width = raw_ref.shape[1]
    for h in range(rows // PART):
        nat[h] = raw_ref[h].astype(F32).reshape(width * PART, cols)
        for x in range(PART):
            row = nat[h, pl.ds(x, width, stride=PART), :]
            flat_ref[:, pl.ds((h * PART + x) * cols, cols)] = row.astype(BF16)

    def fine(x, count):
        return flat_ref[:, pl.ds(x * cols, count * cols)]

    total = None
    for x in range(0, rows, 2):
        term = dot_nt(column_ref[:, pl.ds(x * cols, 2 * cols)], fine(x, 2))
        total = term if total is None else total + term
    own_ref[...] = total
    n1, c1 = plan.counts[1]
    for k in range(rows // 8):
        total = None
        for j in range(4):
            term = dot(fine(8 * k + 2 * j, 2), t1_ref[pl.ds((2 * j + 1) * cols, 2 * cols), :])
            total = term if total is None else total + term
        if k > 0:
            total = total + dot(fine(8 * k - 1, 1), t1_ref[pl.ds(0, cols), :])
        level1[:, pl.ds(4 * k * c1, 4 * c1)] = (total * (1 / 1.5)).astype(BF16)
    level2[...] = (dot(level1[...], t2_ref[...]) * (1 / 1.5)).astype(BF16)


def merge_kernel(plan, count, own_ref, b_ref, a_ref, merge_ref, right_ref, *out_refs):
    even = lax.rem(lax.axis_index("gx"), 2) == 0
    size = plan.row_size
    a, b = a_ref[...], b_ref[...]
    before, after = jnp.where(even, b, a), jnp.where(even, a, b)
    total32 = own_ref[...] + dot(merge_ref[:, :size], before) + dot(merge_ref[:, size:], after)
    total = total32.astype(BF16)
    right_ref[...] = total[: plan.message]
    row = lax.broadcasted_iota(jnp.int32, (plan.edge_size, total.shape[1]), 0)
    tile = jnp.where(row < plan.spare, total32[plan.edge : plan.message], total32[plan.message :])
    right, left = total[plan.edge : plan.message], tile.astype(BF16)
    z = lax.axis_index("gy")
    for step, ref in zip(routes(count), out_refs):
        to_left = chosen(z, [int(step[i] == i - 1) for i in range(count)]) == 1
        ref[: plan.edge] = total[: plan.edge]
        ref[plan.edge :] = jnp.where(to_left, left, right)


def source_of(z, count, d):
    return z if d == 0 else chosen(z, [got[d - 1][1] for got in arrivals(count)])


def local_kernel(
    plan, count, flat_ref, level1, level2, t2_ref, v_ref, k_ref, sa_ref, sb_ref, ra_ref, rb_ref, even_ref, odd_ref,
    first_ref, last_ref, base_ref, spread_ref, carry1,
):
    rows, cols = plan.rows, plan.cols
    n1, c1 = plan.counts[1]
    mixed2 = (dot(v_ref[2], level2[...]) * (1 / 1.5)).astype(BF16)
    step = 4 * c1
    for k in range(n1 * c1 // step):
        lanes = pl.ds(k * step, step)
        mixed1 = dot(v_ref[1], level1[:, lanes]) + dot_nt(mixed2, t2_ref[lanes, :])
        carry1[:, lanes] = (mixed1 * (1 / 1.5)).astype(BF16)

    even = lax.rem(lax.axis_index("gx"), 2) == 0
    a, b = ra_ref[...], rb_ref[...]
    before, after = jnp.where(even, b, a), jnp.where(even, a, b)
    own = jnp.where(even, sa_ref[...], sb_ref[...])
    after = (after.astype(F32) + own.astype(F32)).astype(BF16)

    def mixed_rows(message):
        one = dot_nt(v_ref[1], message) * (1 / 1.5**2)
        two = dot_nt(v_ref[2], message) * (1 / 1.5**4)
        return jnp.concatenate([one, two], axis=1).astype(BF16)

    first, last = mixed_rows(before), mixed_rows(after)
    pairs = rows // 2
    for i in range(pairs):
        lanes = pl.ds(2 * i * cols, 2 * cols)
        total = dot(v_ref[0], flat_ref[:, lanes])
        if i % 2 == 0:
            total = total + dot(carry1[:, pl.ds(i * c1, 2 * c1)], even_ref[...])
        elif i < pairs - 1:
            total = total + dot(carry1[:, pl.ds((i - 1) * c1, 4 * c1)], odd_ref[...])
        else:
            total = total + dot(carry1[:, pl.ds((i - 1) * c1, 2 * c1)], odd_ref[pl.ds(0, 2 * c1), :])
        if i < 2:
            total = total + dot(first, first_ref[:, pl.ds(2 * i * cols, 2 * cols)])
        if i >= pairs - 2:
            total = total + dot(last, last_ref[:, pl.ds(2 * (i - pairs + 2) * cols, 2 * cols)])
        base_ref[:, lanes] = total

    n3, m3 = plan.counts[3][0] + 1, plan.counts[3][1] + 1
    size = k_ref.shape[0]
    block, cells3 = plan.block, plan.cells3
    z = lax.axis_index("gy")

    def parts(shape, dim):
        index = lax.broadcasted_iota(jnp.int32, shape, dim)
        row = jnp.zeros(shape, jnp.int32)
        for r in range(1, n3 + 1):
            row = row + jnp.where(index >= r * m3, 1, 0)
        return row, index - row * m3

    def one(mask):
        return jnp.where(mask, 1.0, 0.0).astype(BF16)

    row, col = parts((size, block), 1)
    place = lax.broadcasted_iota(jnp.int32, (size, block), 0)
    picked = dot(k_ref[...], one((place == z * (m3 - 1) + col) & (row < n3))).astype(BF16)
    source_row, source_col = parts((cells3, block), 0)
    target_row, target_col = parts((cells3, block), 1)
    same = (target_row == source_row) & (target_row < n3)
    target = z * (m3 - 1) + target_col
    _, col = parts((cells3, size), 0)
    place = lax.broadcasted_iota(jnp.int32, (cells3, size), 1)
    for d in range(count):
        start = source_of(z, count, d) * (m3 - 1)
        spread = jnp.where(same, dot(one(place == start + col), picked), 0.0).astype(BF16)
        keep = one(same & (target == start + source_col) & (target < size))
        spread_ref[pl.ds(d * cells3, cells3), :block] = spread
        spread_ref[pl.ds(d * cells3, cells3), block:] = keep


def last_kernel(plan, count, *refs):
    steps = routes(count)
    own_ref, *in_refs = refs[: 1 + len(steps)]
    v_ref, spread_ref, final_ref, base_ref, out_ref, nat, buf, sem = refs[1 + len(steps) :]
    rows, cols = plan.rows, plan.cols
    width = v_ref.shape[1]
    block = plan.block
    z = lax.axis_index("gy")
    messages = [own_ref[...]]
    for d in range(1, count):
        step_of = [got[d - 1][0] for got in arrivals(count)]
        message = None
        for step in sorted(set(step_of)):
            value = in_refs[step][...]
            mine = chosen(z, [int(s == step) for s in step_of]) == 1
            message = value if message is None else jnp.where(mine, value, message)
        messages.append(message)
    level3 = jnp.concatenate([message[: plan.cells3] for message in messages], axis=0)
    mixed = (dot_nt(v_ref[3], level3) * (1 / 1.5**3)).astype(BF16)
    carry = dot(mixed, spread_ref[...])
    carry = (carry[:, :block] + carry[:, block:]) * (1 / 1.5**3)
    left = jnp.zeros((plan.edge_size, width), F32)
    right = own_ref[plan.edge :].astype(F32)
    for d in range(1, count):
        source, edge = source_of(z, count, d), messages[d][plan.edge :].astype(F32)
        left = left + jnp.where((source == z - 1) & (z > 0), edge, 0.0)
        right = right + jnp.where((source == z + 1) & (z < count - 1), edge, 0.0)
    left = left.astype(BF16)
    right = jnp.where(z < count - 1, right, 0.0).astype(BF16)
    edges = jnp.concatenate([left, right], axis=0)
    one = dot_nt(v_ref[1], edges) * (1 / 1.5**2)
    two = dot_nt(v_ref[2], edges) * (1 / 1.5**4)
    parts = jnp.concatenate([carry, one, two], axis=1).astype(BF16)
    copies = []
    for h in range(rows // PART):
        for x in range(0, PART, 2):
            lanes = pl.ds((h * PART + x) * cols, 2 * cols)
            total = base_ref[:, lanes] + dot(parts, final_ref[:, lanes])
            nat[h, pl.ds(x, width, stride=PART), :] = total[:, :cols]
            nat[h, pl.ds(x + 1, width, stride=PART), :] = total[:, cols:]
        buf[h] = nat[h].reshape(width, PART, cols).astype(BF16)
        copy = pltpu.make_async_copy(buf.at[h], out_ref.at[:, pl.ds(h * PART, PART), :], sem.at[h])
        copy.start()
        copies.append(copy)
    for copy in copies:
        copy.wait()


LIMIT = 14 * 1024 * 1024


def call(kernel, ins, outs, scratch=(), hbm=(), any_out=(), name=None, cost=None):
    specs = [pl.BlockSpec(memory_space=pl.ANY if i in hbm else VMEM) for i in range(len(ins))]
    out_specs = [pl.BlockSpec(memory_space=pl.ANY if i in any_out else VMEM) for i in range(len(outs))]
    out_shape = [
        jax.ShapeDtypeStruct(s, t) if i in any_out else VMEM(s, t) for i, (s, t) in enumerate(outs)
    ]
    ins = [pltpu.with_memory_space_constraint(x, pltpu.HBM if i in hbm else VMEM) for i, x in enumerate(ins)]
    return pl.pallas_call(
        kernel,
        in_specs=specs,
        out_specs=out_specs,
        out_shape=out_shape,
        scratch_shapes=list(scratch),
        compiler_params=pltpu.CompilerParams(vmem_limit_bytes=LIMIT),
        cost_estimate=cost,
        name=name,
    )(*ins)


def solution(mesh):
    across, along = mesh.shape["gx"], mesh.shape["gy"]

    def swap(x, first):
        def partner(i):
            return i ^ 1 if first else (i + 1 if i % 2 else i - 1) % across

        return lax.ppermute(x, "gx", [(i, partner(i)) for i in range(across)])

    def on_device(gradient, vertical, kernel):
        width, rows, cols = gradient.shape
        plan = Plan(rows, cols)
        parts = rows // PART
        n1, c1 = plan.counts[1]
        n2, c2 = plan.counts[2]
        size = rows * cols
        row_message = ((plan.row_size, width), BF16)
        cells = plan.cells
        raw, send_a, send_b, column, to_level1, to_level2 = call(
            lambda *refs: first_kernel(plan, *refs),
            [gradient],
            [
                ((parts, width, PART, cols), BF16), row_message, row_message,
                ((cells, size), BF16), ((9 * cols, 4 * c1), BF16), ((n1 * c1, n2 * c2), BF16),
            ],
            [
                VMEM((CHUNKS, 2, width // CHUNKS * PART, cols), F32),
                VMEM((2, width, 3 * cols), BF16), VMEM((plan.row_size, 3 * cols), BF16),
                pltpu.SemaphoreType.DMA((2 * CHUNKS + parts - 2,)),
            ],
            hbm=(0,),
            name="first",
        )
        recv_b = swap(send_b, False)
        recv_a = swap(send_a, True)
        flat, own, level1, level2 = call(
            lambda *refs: inner_kernel(plan, *refs),
            [raw, column, to_level1, to_level2],
            [
                ((width, size), BF16), ((cells, width), F32), ((width, n1 * c1), BF16),
                ((width, n2 * c2), BF16),
            ],
            [VMEM((parts, width * PART, cols), F32)],
            name="inner",
            cost=pl.CostEstimate(flops=3 * cells * width * size, bytes_accessed=4 * 1024 * 1024, transcendentals=0),
        )
        steps = routes(along)
        message = ((plan.message, width), BF16)
        right, *messages = call(
            lambda *refs: merge_kernel(plan, along, *refs),
            [own, recv_b, recv_a, const(plan.merge)],
            [message] * (1 + len(steps)),
            name="merge",
        )
        arrived = [lax.ppermute(x, "gy", list(enumerate(step))) for x, step in zip(messages, steps)]
        base, spread = call(
            lambda *refs: local_kernel(plan, along, *refs),
            [
                flat, level1, level2, to_level2, vertical, kernel, send_a, send_b, recv_a, recv_b, const(plan.even),
                const(plan.odd), const(plan.from_first), const(plan.from_last),
            ],
            [((width, size), F32), ((along * plan.cells3, 2 * plan.block), BF16)],
            [VMEM((width, n1 * c1), BF16)],
            name="local",
            cost=pl.CostEstimate(flops=4 * width * width * size, bytes_accessed=8 * 1024 * 1024, transcendentals=0),
        )
        (out,) = call(
            lambda *refs: last_kernel(plan, along, *refs),
            [right, *arrived, vertical, spread, const(plan.final), base],
            [((width, rows, cols), BF16)],
            [
                VMEM((parts, width * PART, cols), F32),
                VMEM((parts, width, PART, cols), BF16),
                pltpu.SemaphoreType.DMA((parts,)),
            ],
            any_out=(0,),
            name="last",
        )
        return out

    spec = P(None, "gx", "gy")
    return jax.shard_map(on_device, mesh=mesh, in_specs=(spec, P(), P()), out_specs=spec, check_vma=False)
```

```python
import jax
import jax.numpy as jnp
import ml_dtypes
import numpy as np
from jax import lax
from jax.experimental import pallas as pl
from jax.experimental.pallas import tpu as pltpu
from jax.sharding import PartitionSpec as P

BF16 = jnp.bfloat16
F32 = jnp.float32
PART = 8
CHUNKS = 2
VMEM = pltpu.VMEM


def hat(level, fine, cell):
    size = 2**level
    return np.maximum(0.0, 1.0 - np.abs(fine - size * cell) / size)


def weights(level, xs, ys, cell_x, cell_y):
    wx = hat(level, np.asarray(xs)[:, None], np.asarray(cell_x)[None, :])
    wy = hat(level, np.asarray(ys)[:, None], np.asarray(cell_y)[None, :])
    return (wx[:, None, :] * wy[None, :, :]).reshape(len(xs) * len(ys), len(cell_x))


def routes(count):
    if count == 4:
        return [(2, 3, 1, 0), (3, 2, 0, 1), (1, 0, 3, 2)]
    return [[(i + d) % count for i in range(count)] for d in range(1, count)]


def arrivals(count):
    return [
        [(k, step.index(z)) for k, step in enumerate(routes(count)) if step[z] != z] for z in range(count)
    ]


def chosen(index, values):
    result = index * 0
    for i, value in enumerate(values):
        result = result + jnp.where(index == i, value, 0)
    return result


def up16(n):
    return -(-n // 16) * 16


class Plan:
    def __init__(self, rows, cols):
        self.rows, self.cols = rows, cols
        ys = range(cols)
        counts = [(rows >> k, cols >> k) for k in range(4)]
        self.counts = counts
        row_cells = [(k, c) for k in (1, 2, 3) for c in range(counts[k][1] + 1)]
        self.row_cells = row_cells
        self.row_size = up16(len(row_cells))
        assert self.row_size == 128
        n3, m3 = counts[3][0] + 1, counts[3][1] + 1
        self.cells3 = up16(n3 * m3)
        self.block = -(-n3 * m3 // 128) * 128
        self.edge = (n3 * m3) // 16 * 16
        self.spare = n3 * m3 - self.edge
        level3 = [(3, r, c) for r in range(n3) for c in range(m3)]
        edge = [(k, r) for k in (1, 2) for r in range(counts[k][0] + 1)]
        self.message = up16(len(level3) + len(edge))
        self.edge_size = self.message - self.edge
        cells = []
        for side in (1, 0):
            part = [(k, r, side * counts[k][1]) for k, r in edge]
            part = (level3[self.edge :] if side else [None] * self.spare) + part
            cells += (level3[: self.edge] if side else []) + part + [None] * (self.edge_size - len(part))
        cells += [None] * (-len(cells) % 16)
        self.cells = len(cells)

        def table(cells, xs):
            out = np.zeros((len(cells), len(xs) * cols))
            for k in (1, 2, 3):
                where = [i for i, cell in enumerate(cells) if cell is not None and cell[0] == k]
                at = [cells[i] for i in where]
                out[where] = weights(k, xs, ys, [c[1] for c in at], [c[2] for c in at]).T
            return out

        self.cell_list = cells
        merge = np.zeros((len(cells), 2 * self.row_size))
        for i, cell in enumerate(cells):
            if cell is None:
                continue
            k, r, c = cell
            if r == 0:
                merge[i, row_cells.index((k, c))] = 1
            if r == counts[k][0]:
                merge[i, self.row_size + row_cells.index((k, c))] = 1
        self.merge = merge
        c1 = counts[1][1]
        grid = lambda n, m: (np.repeat(np.arange(n), m), np.tile(np.arange(m), n))
        self.even = weights(1, range(0, 2), ys, *grid(2, c1)).T
        self.odd = weights(1, range(2, 4), ys, *grid(4, c1)).T
        def from_row(xs, ends):
            out = np.zeros((2 * self.row_size, 4 * cols))
            for i, (k, c) in enumerate(row_cells):
                if k < 3 and c < counts[k][1]:
                    out[(k - 1) * self.row_size + i] = weights(k, xs, ys, [ends[k]], [c])[:, 0]
            return out

        self.from_first = from_row(range(0, 4), (0, 0, 0))
        self.from_last = from_row(range(rows - 4, rows), [n for n, _ in counts])
        final = [c for c in level3] + [None] * (self.block - len(level3))
        for k in (1, 2):
            for side in (0, 1):
                part = [None] * self.spare
                for level, r in edge:
                    part.append((k, r, side * counts[k][1]) if level == k else None)
                final += part + [None] * (self.edge_size - len(part))
        self.final_size = len(final)
        self.final = table(final, range(rows))


def const(table):
    return jnp.asarray(np.asarray(table).astype(ml_dtypes.bfloat16))


def dot(a, b):
    return jnp.dot(a, b, preferred_element_type=F32)


def dot_nt(a, b):
    return lax.dot_general(a, b, (((1,), (1,)), ((), ())), preferred_element_type=F32)


def ramp(size, offset):
    return jnp.maximum(0, size - jnp.abs(offset))


def cell_tables(cells, shape):
    index = lax.broadcasted_iota(jnp.int32, shape, 0)
    width, first, second = index * 0, index * 0, index * 0
    at = 0
    while at < len(cells):
        if cells[at] is None:
            at += 1
            continue
        k, r, c = cells[at]
        stop = at + 1
        step = None
        while stop < len(cells) and cells[stop] is not None and cells[stop][0] == k:
            move = (cells[stop][1] - cells[stop - 1][1], cells[stop][2] - cells[stop - 1][2])
            if step is None and move in ((0, 1), (1, 0)):
                step = move
            if move != step:
                break
            stop += 1
        step = step or (0, 0)
        mine = (index >= at) & (index < stop)
        width = jnp.where(mine, 2**k, width)
        first = jnp.where(mine, r + step[0] * (index - at), first)
        second = jnp.where(mine, c + step[1] * (index - at), second)
        at = stop
    return width, first, second


def split(index, size, count):
    high = index * 0
    for i in range(1, count):
        high = high + jnp.where(index >= i * size, 1, 0)
    return high, index - high * size


def first_kernel(plan, x_ref, raw_ref, a_ref, b_ref, column_ref, t1_ref, t2_ref, nat, sums, table, sem):
    rows, cols = plan.rows, plan.cols
    width = x_ref.shape[0]
    last = rows // PART - 1
    chunk = width // CHUNKS

    def fetch(h, start, count, i):
        fields = pl.ds(start, count)
        return pltpu.make_async_copy(x_ref.at[fields, pl.ds(h * PART, PART), :], raw_ref.at[h, fields], sem.at[i])

    copies = [
        [fetch(h, c * chunk, chunk, 2 * c + place) for place, h in enumerate((0, last))] for c in range(CHUNKS)
    ]
    copies.append([fetch(h, 0, width, 2 * CHUNKS + h - 1) for h in range(1, last)])
    for group in copies:
        for copy in group:
            copy.start()
    even = lax.rem(lax.axis_index("gx"), 2) == 0

    shape = (plan.cells, cols)
    size, first, second = cell_tables(plan.cell_list, shape)
    y = lax.broadcasted_iota(jnp.int32, shape, 1)
    inverse = jnp.where(size == 2, 0.25, jnp.where(size == 4, 0.0625, 0.015625))
    along = ramp(size, y - size * second).astype(F32) * inverse
    size, start = size.astype(F32), (size * first).astype(F32)
    for x in range(rows):
        column_ref[:, pl.ds(x * cols, cols)] = (ramp(size, start - x) * along).astype(BF16)
    n1, c1 = plan.counts[1]
    n2, c2 = plan.counts[2]
    shape = (cols, 4 * c1)
    i, c = split(lax.broadcasted_iota(jnp.int32, shape, 1), c1, 4)
    along = ramp(2, lax.broadcasted_iota(jnp.int32, shape, 0) - 2 * c).astype(F32) * 0.25
    i = 2 * i[:1]
    for x in range(9):
        t1_ref[pl.ds(x * cols, cols), :] = (ramp(2, i - (x - 1)).astype(F32) * along).astype(BF16)
    shape = (c1, n2 * c2)
    i, c = split(lax.broadcasted_iota(jnp.int32, shape, 1), c2, n2)
    along = ramp(2, lax.broadcasted_iota(jnp.int32, shape, 0) - 2 * c).astype(F32) * 0.25
    i = 2 * i[:1]
    for x in range(n1):
        t2_ref[pl.ds(x * c1, c1), :] = (ramp(2, i - x).astype(F32) * along).astype(BF16)
    shape = (plan.row_size, cols)
    level, _, second = cell_tables([(k, 0, c) for k, c in plan.row_cells], shape)
    y = lax.broadcasted_iota(jnp.int32, shape, 1)
    for k in (1, 2, 3):
        weight = ramp(2**k, y - 2**k * second).astype(F32) * 0.5**k
        table[:, pl.ds((k - 1) * cols, cols)] = jnp.where(level == 2**k, weight, 0.0).astype(BF16)
    for c in range(CHUNKS):
        fields = pl.ds(c * chunk, chunk)
        for place, (h, end) in enumerate(((0, 0), (last, PART))):
            copies[c][place].wait()
            nat[c, place] = raw_ref[h, fields].astype(F32).reshape(chunk * PART, cols)
            found = [None] * 3
            for x in range(PART):
                row = nat[c, place, pl.ds(x, chunk, stride=PART), :]
                for k in range(3):
                    weight = float(hat(k + 1, x, end / 2 ** (k + 1)))
                    if weight:
                        term = row * weight
                        found[k] = term if found[k] is None else found[k] + term
            for k in range(3):
                sums[place, fields, pl.ds(k * cols, cols)] = found[k].astype(BF16)
    low, up = [dot_nt(table[...], sums[place]).astype(BF16) for place in range(2)]
    a_ref[...] = jnp.where(even, up, low)
    b_ref[...] = jnp.where(even, low, up)
    for copy in copies[-1]:
        copy.wait()


def inner_kernel(
    plan, raw_ref, column_ref, t1_ref, t2_ref, flat_ref, own_ref, level1, level2, nat
):
    rows, cols = plan.rows, plan.cols
    width = raw_ref.shape[1]
    for h in range(rows // PART):
        nat[h] = raw_ref[h].astype(F32).reshape(width * PART, cols)
        for x in range(PART):
            row = nat[h, pl.ds(x, width, stride=PART), :]
            flat_ref[:, pl.ds((h * PART + x) * cols, cols)] = row.astype(BF16)

    def fine(x, count):
        return flat_ref[:, pl.ds(x * cols, count * cols)]

    total = None
    for x in range(0, rows, 2):
        term = dot_nt(column_ref[:, pl.ds(x * cols, 2 * cols)], fine(x, 2))
        total = term if total is None else total + term
    own_ref[...] = total
    n1, c1 = plan.counts[1]
    for k in range(rows // 8):
        total = None
        for j in range(4):
            term = dot(fine(8 * k + 2 * j, 2), t1_ref[pl.ds((2 * j + 1) * cols, 2 * cols), :])
            total = term if total is None else total + term
        if k > 0:
            total = total + dot(fine(8 * k - 1, 1), t1_ref[pl.ds(0, cols), :])
        level1[:, pl.ds(4 * k * c1, 4 * c1)] = (total * (1 / 1.5)).astype(BF16)
    level2[...] = (dot(level1[...], t2_ref[...]) * (1 / 1.5)).astype(BF16)


def merge_kernel(plan, count, own_ref, b_ref, a_ref, merge_ref, right_ref, *out_refs):
    even = lax.rem(lax.axis_index("gx"), 2) == 0
    a, b = a_ref[...], b_ref[...]
    before, after = jnp.where(even, b, a), jnp.where(even, a, b)
    total32 = own_ref[...] + dot(merge_ref[...], jnp.concatenate([before, after], axis=0))
    total = total32.astype(BF16)
    right_ref[...] = total[: plan.message]
    row = lax.broadcasted_iota(jnp.int32, (plan.edge_size, total.shape[1]), 0)
    tile = jnp.where(row < plan.spare, total32[plan.edge : plan.message], total32[plan.message :])
    right, left = total[plan.edge : plan.message], tile.astype(BF16)
    z = lax.axis_index("gy")
    for step, ref in zip(routes(count), out_refs):
        to_left = chosen(z, [int(step[i] == i - 1) for i in range(count)]) == 1
        ref[: plan.edge] = total[: plan.edge]
        ref[plan.edge :] = jnp.where(to_left, left, right)


def source_of(z, count, d):
    return z if d == 0 else chosen(z, [got[d - 1][1] for got in arrivals(count)])


def local_kernel(
    plan, count, flat_ref, level1, level2, t2_ref, v_ref, k_ref, sa_ref, sb_ref, ra_ref, rb_ref, even_ref, odd_ref,
    first_ref, last_ref, base_ref, spread_ref, carry1,
):
    rows, cols = plan.rows, plan.cols
    n1, c1 = plan.counts[1]
    mixed2 = (dot(v_ref[2], level2[...]) * (1 / 1.5)).astype(BF16)
    step = 4 * c1
    for k in range(n1 * c1 // step):
        lanes = pl.ds(k * step, step)
        mixed1 = dot(v_ref[1], level1[:, lanes]) + dot_nt(mixed2, t2_ref[lanes, :])
        carry1[:, lanes] = (mixed1 * (1 / 1.5)).astype(BF16)

    even = lax.rem(lax.axis_index("gx"), 2) == 0
    a, b = ra_ref[...], rb_ref[...]
    before, after = jnp.where(even, b, a), jnp.where(even, a, b)
    own = jnp.where(even, sa_ref[...], sb_ref[...])
    after = (after.astype(F32) + own.astype(F32)).astype(BF16)

    def mixed_rows(message):
        one = dot_nt(v_ref[1], message) * (1 / 1.5**2)
        two = dot_nt(v_ref[2], message) * (1 / 1.5**4)
        return jnp.concatenate([one, two], axis=1).astype(BF16)

    first, last = mixed_rows(before), mixed_rows(after)
    pairs = rows // 2
    for i in range(pairs):
        lanes = pl.ds(2 * i * cols, 2 * cols)
        total = dot(v_ref[0], flat_ref[:, lanes])
        if i % 2 == 0:
            total = total + dot(carry1[:, pl.ds(i * c1, 2 * c1)], even_ref[...])
        elif i < pairs - 1:
            total = total + dot(carry1[:, pl.ds((i - 1) * c1, 4 * c1)], odd_ref[...])
        else:
            total = total + dot(carry1[:, pl.ds((i - 1) * c1, 2 * c1)], odd_ref[pl.ds(0, 2 * c1), :])
        if i < 2:
            total = total + dot(first, first_ref[:, pl.ds(2 * i * cols, 2 * cols)])
        if i >= pairs - 2:
            total = total + dot(last, last_ref[:, pl.ds(2 * (i - pairs + 2) * cols, 2 * cols)])
        base_ref[:, lanes] = total

    n3, m3 = plan.counts[3][0] + 1, plan.counts[3][1] + 1
    size = k_ref.shape[0]
    block, cells3 = plan.block, plan.cells3
    z = lax.axis_index("gy")

    def parts(shape, dim):
        index = lax.broadcasted_iota(jnp.int32, shape, dim)
        row = jnp.zeros(shape, jnp.int32)
        for r in range(1, n3 + 1):
            row = row + jnp.where(index >= r * m3, 1, 0)
        return row, index - row * m3

    def one(mask):
        return jnp.where(mask, 1.0, 0.0).astype(BF16)

    row, col = parts((size, block), 1)
    place = lax.broadcasted_iota(jnp.int32, (size, block), 0)
    picked = dot(k_ref[...], one((place == z * (m3 - 1) + col) & (row < n3))).astype(BF16)
    source_row, source_col = parts((cells3, block), 0)
    target_row, target_col = parts((cells3, block), 1)
    same = (target_row == source_row) & (target_row < n3)
    target = z * (m3 - 1) + target_col
    _, col = parts((cells3, size), 0)
    place = lax.broadcasted_iota(jnp.int32, (cells3, size), 1)
    for d in range(count):
        start = source_of(z, count, d) * (m3 - 1)
        spread = jnp.where(same, dot(one(place == start + col), picked), 0.0).astype(BF16)
        keep = one(same & (target == start + source_col) & (target < size))
        spread_ref[pl.ds(d * cells3, cells3), :block] = spread
        spread_ref[pl.ds(d * cells3, cells3), block:] = keep


def column_parts(plan, count, messages, first, v_ref, spread_ref):
    width = v_ref.shape[1]
    block, cells3 = plan.block, plan.cells3
    z = lax.axis_index("gy")
    level3 = jnp.concatenate([message[:cells3] for message in messages], axis=0)
    mixed = (dot_nt(v_ref[3], level3) * (1 / 1.5**3)).astype(BF16)
    carry = dot(mixed, spread_ref[pl.ds(first * cells3, len(messages) * cells3), :])
    carry = (carry[:, :block] + carry[:, block:]) * (1 / 1.5**3)
    left = jnp.zeros((plan.edge_size, width), F32)
    right = jnp.zeros((plan.edge_size, width), F32)
    for d, message in enumerate(messages, first):
        source, edge = source_of(z, count, d), message[plan.edge :].astype(F32)
        if d == 0:
            right = right + edge
        else:
            left = left + jnp.where((source == z - 1) & (z > 0), edge, 0.0)
            right = right + jnp.where(source == z + 1, edge, 0.0)
    right = jnp.where(z < count - 1, right, 0.0)
    edges = jnp.concatenate([left, right], axis=0).astype(BF16)
    one = dot_nt(v_ref[1], edges) * (1 / 1.5**2)
    two = dot_nt(v_ref[2], edges) * (1 / 1.5**4)
    return jnp.concatenate([carry, one, two], axis=1)


def gather_kernel(plan, count, *refs):
    *message_refs, v_ref, spread_ref, parts_ref = refs
    parts_ref[...] = column_parts(plan, count, [ref[...] for ref in message_refs], 0, v_ref, spread_ref)


def last_kernel(plan, count, in_ref, parts_ref, v_ref, spread_ref, final_ref, base_ref, out_ref, nat, buf, sem):
    rows, cols = plan.rows, plan.cols
    width = v_ref.shape[1]
    parts = column_parts(plan, count, [in_ref[...]], count - 1, v_ref, spread_ref)
    parts = (parts + parts_ref[...]).astype(BF16)
    copies = []
    for h in range(rows // PART):
        for x in range(0, PART, 2):
            lanes = pl.ds((h * PART + x) * cols, 2 * cols)
            total = base_ref[:, lanes] + dot(parts, final_ref[:, lanes])
            nat[h, pl.ds(x, width, stride=PART), :] = total[:, :cols]
            nat[h, pl.ds(x + 1, width, stride=PART), :] = total[:, cols:]
        pieces = CHUNKS if h == rows // PART - 1 else 1
        part = width // pieces
        for i in range(pieces):
            fields = pl.ds(i * part, part)
            found = nat[h, pl.ds(i * part * PART, part * PART), :]
            buf[h, fields] = found.reshape(part, PART, cols).astype(BF16)
            copy = pltpu.make_async_copy(
                buf.at[h, fields], out_ref.at[fields, pl.ds(h * PART, PART), :], sem.at[h + i]
            )
            copy.start()
            copies.append(copy)
    for copy in copies:
        copy.wait()


LIMIT = 14 * 1024 * 1024


def call(kernel, ins, outs, scratch=(), hbm=(), any_out=(), name=None, cost=None):
    specs = [pl.BlockSpec(memory_space=pl.ANY if i in hbm else VMEM) for i in range(len(ins))]
    out_specs = [pl.BlockSpec(memory_space=pl.ANY if i in any_out else VMEM) for i in range(len(outs))]
    out_shape = [
        jax.ShapeDtypeStruct(s, t) if i in any_out else VMEM(s, t) for i, (s, t) in enumerate(outs)
    ]
    ins = [pltpu.with_memory_space_constraint(x, pltpu.HBM if i in hbm else VMEM) for i, x in enumerate(ins)]
    return pl.pallas_call(
        kernel,
        in_specs=specs,
        out_specs=out_specs,
        out_shape=out_shape,
        scratch_shapes=list(scratch),
        compiler_params=pltpu.CompilerParams(vmem_limit_bytes=LIMIT),
        cost_estimate=cost,
        name=name,
    )(*ins)


def solution(mesh):
    across, along = mesh.shape["gx"], mesh.shape["gy"]

    def swap(x, first):
        def partner(i):
            return i ^ 1 if first else (i + 1 if i % 2 else i - 1) % across

        return lax.ppermute(x, "gx", [(i, partner(i)) for i in range(across)])

    def on_device(gradient, vertical, kernel):
        width, rows, cols = gradient.shape
        plan = Plan(rows, cols)
        parts = rows // PART
        n1, c1 = plan.counts[1]
        n2, c2 = plan.counts[2]
        size = rows * cols
        row_message = ((plan.row_size, width), BF16)
        cells = plan.cells
        raw, send_a, send_b, column, to_level1, to_level2 = call(
            lambda *refs: first_kernel(plan, *refs),
            [gradient],
            [
                ((parts, width, PART, cols), BF16), row_message, row_message,
                ((cells, size), BF16), ((9 * cols, 4 * c1), BF16), ((n1 * c1, n2 * c2), BF16),
            ],
            [
                VMEM((CHUNKS, 2, width // CHUNKS * PART, cols), F32),
                VMEM((2, width, 3 * cols), BF16), VMEM((plan.row_size, 3 * cols), BF16),
                pltpu.SemaphoreType.DMA((2 * CHUNKS + parts - 2,)),
            ],
            hbm=(0,),
            name="first",
        )
        recv_b = swap(send_b, False)
        recv_a = swap(send_a, True)
        flat, own, level1, level2 = call(
            lambda *refs: inner_kernel(plan, *refs),
            [raw, column, to_level1, to_level2],
            [
                ((width, size), BF16), ((cells, width), F32), ((width, n1 * c1), BF16),
                ((width, n2 * c2), BF16),
            ],
            [VMEM((parts, width * PART, cols), F32)],
            name="inner",
            cost=pl.CostEstimate(flops=3 * cells * width * size, bytes_accessed=4 * 1024 * 1024, transcendentals=0),
        )
        steps = routes(along)
        message = ((plan.message, width), BF16)
        right, *messages = call(
            lambda *refs: merge_kernel(plan, along, *refs),
            [own, recv_b, recv_a, const(plan.merge)],
            [message] * (1 + len(steps)),
            name="merge",
        )
        arrived = [lax.ppermute(x, "gy", list(enumerate(step))) for x, step in zip(messages, steps)]
        base, spread = call(
            lambda *refs: local_kernel(plan, along, *refs),
            [
                flat, level1, level2, to_level2, vertical, kernel, send_a, send_b, recv_a, recv_b, const(plan.even),
                const(plan.odd), const(plan.from_first), const(plan.from_last),
            ],
            [((width, size), F32), ((along * plan.cells3, 2 * plan.block), BF16)],
            [VMEM((width, n1 * c1), BF16)],
            name="local",
            cost=pl.CostEstimate(flops=4 * width * width * size, bytes_accessed=8 * 1024 * 1024, transcendentals=0),
        )
        (partial,) = call(
            lambda *refs: gather_kernel(plan, along, *refs),
            [right, *arrived[:-1], vertical, spread],
            [((width, plan.final_size), F32)],
            name="gather",
        )
        (out,) = call(
            lambda *refs: last_kernel(plan, along, *refs),
            [arrived[-1], partial, vertical, spread, const(plan.final), base],
            [((width, rows, cols), BF16)],
            [
                VMEM((parts, width * PART, cols), F32),
                VMEM((parts, width, PART, cols), BF16),
                pltpu.SemaphoreType.DMA((parts + CHUNKS - 1,)),
            ],
            any_out=(0,),
            name="last",
        )
        return out

    spec = P(None, "gx", "gy")
    return jax.shard_map(on_device, mesh=mesh, in_specs=(spec, P(), P()), out_specs=spec, check_vma=False)
```

```python
import jax
import jax.numpy as jnp
import ml_dtypes
import numpy as np
from jax import lax
from jax.experimental import pallas as pl
from jax.experimental.pallas import tpu as pltpu
from jax.sharding import PartitionSpec as P

BF16 = jnp.bfloat16
F32 = jnp.float32
PART = 8
CHUNKS = 2
VMEM = pltpu.VMEM


def hat(level, fine, cell):
    size = 2**level
    return np.maximum(0.0, 1.0 - np.abs(fine - size * cell) / size)


def weights(level, xs, ys, cell_x, cell_y):
    wx = hat(level, np.asarray(xs)[:, None], np.asarray(cell_x)[None, :])
    wy = hat(level, np.asarray(ys)[:, None], np.asarray(cell_y)[None, :])
    return (wx[:, None, :] * wy[None, :, :]).reshape(len(xs) * len(ys), len(cell_x))


def routes(count):
    if count == 4:
        return [(2, 3, 1, 0), (3, 2, 0, 1), (1, 0, 3, 2)]
    return [[(i + d) % count for i in range(count)] for d in range(1, count)]


def arrivals(count):
    return [
        [(k, step.index(z)) for k, step in enumerate(routes(count)) if step[z] != z] for z in range(count)
    ]


def chosen(index, values):
    result = index * 0
    for i, value in enumerate(values):
        result = result + jnp.where(index == i, value, 0)
    return result


def up16(n):
    return -(-n // 16) * 16


class Plan:
    def __init__(self, rows, cols):
        self.rows, self.cols = rows, cols
        ys = range(cols)
        counts = [(rows >> k, cols >> k) for k in range(4)]
        self.counts = counts
        row_cells = [(k, c) for k in (1, 2, 3) for c in range(counts[k][1] + 1)]
        self.row_cells = row_cells
        self.row_size = up16(len(row_cells))
        assert self.row_size == 128
        n3, m3 = counts[3][0] + 1, counts[3][1] + 1
        self.cells3 = up16(n3 * m3)
        self.block = -(-n3 * m3 // 128) * 128
        self.edge = (n3 * m3) // 16 * 16
        self.spare = n3 * m3 - self.edge
        level3 = [(3, r, c) for r in range(n3) for c in range(m3)]
        edge = [(k, r) for k in (1, 2) for r in range(counts[k][0] + 1)]
        self.message = up16(len(level3) + len(edge))
        self.edge_size = self.message - self.edge
        cells = []
        for side in (1, 0):
            part = [(k, r, side * counts[k][1]) for k, r in edge]
            part = (level3[self.edge :] if side else [None] * self.spare) + part
            cells += (level3[: self.edge] if side else []) + part + [None] * (self.edge_size - len(part))
        cells += [None] * (-len(cells) % 16)
        self.cells = len(cells)

        def table(cells, xs):
            out = np.zeros((len(cells), len(xs) * cols))
            for k in (1, 2, 3):
                where = [i for i, cell in enumerate(cells) if cell is not None and cell[0] == k]
                at = [cells[i] for i in where]
                out[where] = weights(k, xs, ys, [c[1] for c in at], [c[2] for c in at]).T
            return out

        self.cell_list = cells
        merge = np.zeros((len(cells), 2 * self.row_size))
        for i, cell in enumerate(cells):
            if cell is None:
                continue
            k, r, c = cell
            if r == 0:
                merge[i, row_cells.index((k, c))] = 1
            if r == counts[k][0]:
                merge[i, self.row_size + row_cells.index((k, c))] = 1
        self.merge = merge
        c1 = counts[1][1]
        grid = lambda n, m: (np.repeat(np.arange(n), m), np.tile(np.arange(m), n))
        self.even = weights(1, range(0, 2), ys, *grid(2, c1)).T
        self.odd = weights(1, range(2, 4), ys, *grid(4, c1)).T
        def from_row(xs, ends):
            out = np.zeros((2 * self.row_size, 4 * cols))
            for i, (k, c) in enumerate(row_cells):
                if k < 3 and c < counts[k][1]:
                    out[(k - 1) * self.row_size + i] = weights(k, xs, ys, [ends[k]], [c])[:, 0]
            return out

        self.from_first = from_row(range(0, 4), (0, 0, 0))
        self.from_last = from_row(range(rows - 4, rows), [n for n, _ in counts])
        final = [c for c in level3] + [None] * (self.block - len(level3))
        for k in (1, 2):
            for side in (0, 1):
                part = [None] * self.spare
                for level, r in edge:
                    part.append((k, r, side * counts[k][1]) if level == k else None)
                final += part + [None] * (self.edge_size - len(part))
        self.final_size = len(final)
        self.final = table(final, range(rows))


def const(table):
    return jnp.asarray(np.asarray(table).astype(ml_dtypes.bfloat16))


def dot(a, b):
    return jnp.dot(a, b, preferred_element_type=F32)


def dot_nt(a, b):
    return lax.dot_general(a, b, (((1,), (1,)), ((), ())), preferred_element_type=F32)


def ramp(size, offset):
    return jnp.maximum(0, size - jnp.abs(offset))


def cell_tables(cells, shape):
    index = lax.broadcasted_iota(jnp.int32, shape, 0)
    width, first, second = index * 0, index * 0, index * 0
    at = 0
    while at < len(cells):
        if cells[at] is None:
            at += 1
            continue
        k, r, c = cells[at]
        stop = at + 1
        step = None
        while stop < len(cells) and cells[stop] is not None and cells[stop][0] == k:
            move = (cells[stop][1] - cells[stop - 1][1], cells[stop][2] - cells[stop - 1][2])
            if step is None and move in ((0, 1), (1, 0)):
                step = move
            if move != step:
                break
            stop += 1
        step = step or (0, 0)
        mine = (index >= at) & (index < stop)
        width = jnp.where(mine, 2**k, width)
        first = jnp.where(mine, r + step[0] * (index - at), first)
        second = jnp.where(mine, c + step[1] * (index - at), second)
        at = stop
    return width, first, second


def split(index, size, count):
    high = index * 0
    for i in range(1, count):
        high = high + jnp.where(index >= i * size, 1, 0)
    return high, index - high * size


def first_kernel(plan, x_ref, raw_ref, a_ref, b_ref, column_ref, t1_ref, t2_ref, nat, sums, table, sem):
    rows, cols = plan.rows, plan.cols
    width = x_ref.shape[0]
    last = rows // PART - 1
    chunk = width // CHUNKS

    def fetch(h, start, count, i):
        fields = pl.ds(start, count)
        return pltpu.make_async_copy(x_ref.at[fields, pl.ds(h * PART, PART), :], raw_ref.at[h, fields], sem.at[i])

    copies = [
        [fetch(h, c * chunk, chunk, 2 * c + place) for place, h in enumerate((0, last))] for c in range(CHUNKS)
    ]
    copies.append([fetch(h, 0, width, 2 * CHUNKS + h - 1) for h in range(1, last)])
    for group in copies:
        for copy in group:
            copy.start()
    even = lax.rem(lax.axis_index("gx"), 2) == 0

    shape = (plan.cells, cols)
    size, first, second = cell_tables(plan.cell_list, shape)
    y = lax.broadcasted_iota(jnp.int32, shape, 1)
    inverse = jnp.where(size == 2, 0.25, jnp.where(size == 4, 0.0625, 0.015625))
    along = ramp(size, y - size * second).astype(F32) * inverse
    size, start = size.astype(F32), (size * first).astype(F32)
    for x in range(rows):
        column_ref[:, pl.ds(x * cols, cols)] = (ramp(size, start - x) * along).astype(BF16)
    n1, c1 = plan.counts[1]
    n2, c2 = plan.counts[2]
    shape = (cols, 4 * c1)
    i, c = split(lax.broadcasted_iota(jnp.int32, shape, 1), c1, 4)
    along = ramp(2, lax.broadcasted_iota(jnp.int32, shape, 0) - 2 * c).astype(F32) * 0.25
    i = 2 * i[:1]
    for x in range(9):
        t1_ref[pl.ds(x * cols, cols), :] = (ramp(2, i - (x - 1)).astype(F32) * along).astype(BF16)
    shape = (c1, n2 * c2)
    i, c = split(lax.broadcasted_iota(jnp.int32, shape, 1), c2, n2)
    along = ramp(2, lax.broadcasted_iota(jnp.int32, shape, 0) - 2 * c).astype(F32) * 0.25
    i = 2 * i[:1]
    for x in range(n1):
        t2_ref[pl.ds(x * c1, c1), :] = (ramp(2, i - x).astype(F32) * along).astype(BF16)
    shape = (plan.row_size, cols)
    level, _, second = cell_tables([(k, 0, c) for k, c in plan.row_cells], shape)
    y = lax.broadcasted_iota(jnp.int32, shape, 1)
    for k in (1, 2, 3):
        weight = ramp(2**k, y - 2**k * second).astype(F32) * 0.5**k
        table[:, pl.ds((k - 1) * cols, cols)] = jnp.where(level == 2**k, weight, 0.0).astype(BF16)
    for c in range(CHUNKS):
        fields = pl.ds(c * chunk, chunk)
        for place, (h, end) in enumerate(((0, 0), (last, PART))):
            copies[c][place].wait()
            nat[c, place] = raw_ref[h, fields].astype(F32).reshape(chunk * PART, cols)
            found = [None] * 3
            for x in range(PART):
                row = nat[c, place, pl.ds(x, chunk, stride=PART), :]
                for k in range(3):
                    weight = float(hat(k + 1, x, end / 2 ** (k + 1)))
                    if weight:
                        term = row * weight
                        found[k] = term if found[k] is None else found[k] + term
            for k in range(3):
                sums[place, fields, pl.ds(k * cols, cols)] = found[k].astype(BF16)
    low, up = [dot_nt(table[...], sums[place]).astype(BF16) for place in range(2)]
    a_ref[...] = jnp.where(even, up, low)
    b_ref[...] = jnp.where(even, low, up)
    for copy in copies[-1]:
        copy.wait()


def inner_kernel(
    plan, raw_ref, column_ref, t1_ref, t2_ref, flat_ref, own_ref, level1, level2, nat
):
    rows, cols = plan.rows, plan.cols
    width = raw_ref.shape[1]
    for h in range(rows // PART):
        nat[h] = raw_ref[h].astype(F32).reshape(width * PART, cols)
        for x in range(PART):
            row = nat[h, pl.ds(x, width, stride=PART), :]
            flat_ref[:, pl.ds((h * PART + x) * cols, cols)] = row.astype(BF16)

    def fine(x, count):
        return flat_ref[:, pl.ds(x * cols, count * cols)]

    total = None
    for x in range(0, rows, 2):
        term = dot_nt(column_ref[:, pl.ds(x * cols, 2 * cols)], fine(x, 2))
        total = term if total is None else total + term
    own_ref[...] = total
    n1, c1 = plan.counts[1]
    for k in range(rows // 8):
        total = None
        for j in range(4):
            term = dot(fine(8 * k + 2 * j, 2), t1_ref[pl.ds((2 * j + 1) * cols, 2 * cols), :])
            total = term if total is None else total + term
        if k > 0:
            total = total + dot(fine(8 * k - 1, 1), t1_ref[pl.ds(0, cols), :])
        level1[:, pl.ds(4 * k * c1, 4 * c1)] = (total * (1 / 1.5)).astype(BF16)
    level2[...] = (dot(level1[...], t2_ref[...]) * (1 / 1.5)).astype(BF16)


def merge_kernel(plan, count, own_ref, a_ref, b_ref, merge_ref, right_ref, *out_refs):
    even = lax.rem(lax.axis_index("gx"), 2) == 0
    a, b = a_ref[...], b_ref[...]
    before, after = jnp.where(even, b, a), jnp.where(even, a, b)
    total32 = own_ref[...] + dot(merge_ref[...], jnp.concatenate([before, after], axis=0))
    total = total32.astype(BF16)
    right_ref[...] = total[: plan.message]
    row = lax.broadcasted_iota(jnp.int32, (plan.edge_size, total.shape[1]), 0)
    tile = jnp.where(row < plan.spare, total32[plan.edge : plan.message], total32[plan.message :])
    right, left = total[plan.edge : plan.message], tile.astype(BF16)
    z = lax.axis_index("gy")
    for step, ref in zip(routes(count), out_refs):
        to_left = chosen(z, [int(step[i] == i - 1) for i in range(count)]) == 1
        ref[: plan.edge] = total[: plan.edge]
        ref[plan.edge :] = jnp.where(to_left, left, right)


def source_of(z, count, d):
    return z if d == 0 else chosen(z, [got[d - 1][1] for got in arrivals(count)])


def local_kernel(
    plan, count, flat_ref, level1, level2, t2_ref, v_ref, k_ref, sa_ref, sb_ref, ra_ref, rb_ref, even_ref, odd_ref,
    first_ref, last_ref, base_ref, spread_ref, carry1,
):
    rows, cols = plan.rows, plan.cols
    n1, c1 = plan.counts[1]
    mixed2 = (dot(v_ref[2], level2[...]) * (1 / 1.5)).astype(BF16)
    step = 4 * c1
    for k in range(n1 * c1 // step):
        lanes = pl.ds(k * step, step)
        mixed1 = dot(v_ref[1], level1[:, lanes]) + dot_nt(mixed2, t2_ref[lanes, :])
        carry1[:, lanes] = (mixed1 * (1 / 1.5)).astype(BF16)

    even = lax.rem(lax.axis_index("gx"), 2) == 0
    a, b = ra_ref[...], rb_ref[...]
    before, after = jnp.where(even, b, a), jnp.where(even, a, b)
    own = jnp.where(even, sa_ref[...], sb_ref[...])
    after = (after.astype(F32) + own.astype(F32)).astype(BF16)

    def mixed_rows(message):
        one = dot_nt(v_ref[1], message) * (1 / 1.5**2)
        two = dot_nt(v_ref[2], message) * (1 / 1.5**4)
        return jnp.concatenate([one, two], axis=1).astype(BF16)

    first, last = mixed_rows(before), mixed_rows(after)
    pairs = rows // 2
    for i in range(pairs):
        lanes = pl.ds(2 * i * cols, 2 * cols)
        total = dot(v_ref[0], flat_ref[:, lanes])
        if i % 2 == 0:
            total = total + dot(carry1[:, pl.ds(i * c1, 2 * c1)], even_ref[...])
        elif i < pairs - 1:
            total = total + dot(carry1[:, pl.ds((i - 1) * c1, 4 * c1)], odd_ref[...])
        else:
            total = total + dot(carry1[:, pl.ds((i - 1) * c1, 2 * c1)], odd_ref[pl.ds(0, 2 * c1), :])
        if i < 2:
            total = total + dot(first, first_ref[:, pl.ds(2 * i * cols, 2 * cols)])
        if i >= pairs - 2:
            total = total + dot(last, last_ref[:, pl.ds(2 * (i - pairs + 2) * cols, 2 * cols)])
        base_ref[:, lanes] = total

    n3, m3 = plan.counts[3][0] + 1, plan.counts[3][1] + 1
    size = k_ref.shape[0]
    block, cells3 = plan.block, plan.cells3
    z = lax.axis_index("gy")

    def parts(shape, dim):
        index = lax.broadcasted_iota(jnp.int32, shape, dim)
        row = jnp.zeros(shape, jnp.int32)
        for r in range(1, n3 + 1):
            row = row + jnp.where(index >= r * m3, 1, 0)
        return row, index - row * m3

    def one(mask):
        return jnp.where(mask, 1.0, 0.0).astype(BF16)

    row, col = parts((size, block), 1)
    place = lax.broadcasted_iota(jnp.int32, (size, block), 0)
    picked = dot(k_ref[...], one((place == z * (m3 - 1) + col) & (row < n3))).astype(BF16)
    source_row, source_col = parts((cells3, block), 0)
    target_row, target_col = parts((cells3, block), 1)
    same = (target_row == source_row) & (target_row < n3)
    target = z * (m3 - 1) + target_col
    _, col = parts((cells3, size), 0)
    place = lax.broadcasted_iota(jnp.int32, (cells3, size), 1)
    for d in range(count):
        start = source_of(z, count, d) * (m3 - 1)
        spread = jnp.where(same, dot(one(place == start + col), picked), 0.0).astype(BF16)
        keep = one(same & (target == start + source_col) & (target < size))
        spread_ref[pl.ds(d * cells3, cells3), :block] = spread
        spread_ref[pl.ds(d * cells3, cells3), block:] = keep


def column_parts(plan, count, messages, first, v_ref, spread_ref):
    width = v_ref.shape[1]
    block, cells3 = plan.block, plan.cells3
    z = lax.axis_index("gy")
    level3 = jnp.concatenate([message[:cells3] for message in messages], axis=0)
    mixed = (dot_nt(v_ref[3], level3) * (1 / 1.5**3)).astype(BF16)
    carry = dot(mixed, spread_ref[pl.ds(first * cells3, len(messages) * cells3), :])
    carry = (carry[:, :block] + carry[:, block:]) * (1 / 1.5**3)
    left = jnp.zeros((plan.edge_size, width), F32)
    right = jnp.zeros((plan.edge_size, width), F32)
    for d, message in enumerate(messages, first):
        source, edge = source_of(z, count, d), message[plan.edge :].astype(F32)
        if d == 0:
            right = right + edge
        else:
            left = left + jnp.where((source == z - 1) & (z > 0), edge, 0.0)
            right = right + jnp.where(source == z + 1, edge, 0.0)
    right = jnp.where(z < count - 1, right, 0.0)
    edges = jnp.concatenate([left, right], axis=0).astype(BF16)
    one = dot_nt(v_ref[1], edges) * (1 / 1.5**2)
    two = dot_nt(v_ref[2], edges) * (1 / 1.5**4)
    return jnp.concatenate([carry, one, two], axis=1)


def gather_kernel(plan, count, *refs):
    *message_refs, v_ref, spread_ref, parts_ref = refs
    parts_ref[...] = column_parts(plan, count, [ref[...] for ref in message_refs], 0, v_ref, spread_ref)


def last_kernel(plan, count, in_ref, parts_ref, v_ref, spread_ref, final_ref, base_ref, out_ref, nat, buf, sem):
    rows, cols = plan.rows, plan.cols
    width = v_ref.shape[1]
    parts = column_parts(plan, count, [in_ref[...]], count - 1, v_ref, spread_ref)
    parts = (parts + parts_ref[...]).astype(BF16)
    copies = []
    for h in range(rows // PART):
        lanes = pl.ds(h * PART * cols, PART * cols)
        total = base_ref[:, lanes] + dot(parts, final_ref[:, lanes])
        for x in range(PART):
            nat[h, pl.ds(x, width, stride=PART), :] = total[:, x * cols : (x + 1) * cols]
        pieces = CHUNKS if h == rows // PART - 1 else 1
        part = width // pieces
        for i in range(pieces):
            fields = pl.ds(i * part, part)
            found = nat[h, pl.ds(i * part * PART, part * PART), :]
            buf[h, fields] = found.reshape(part, PART, cols).astype(BF16)
            copy = pltpu.make_async_copy(
                buf.at[h, fields], out_ref.at[fields, pl.ds(h * PART, PART), :], sem.at[h + i]
            )
            copy.start()
            copies.append(copy)
    for copy in copies:
        copy.wait()


LIMIT = 14 * 1024 * 1024


def call(kernel, ins, outs, scratch=(), hbm=(), any_out=(), name=None, cost=None):
    specs = [pl.BlockSpec(memory_space=pl.ANY if i in hbm else VMEM) for i in range(len(ins))]
    out_specs = [pl.BlockSpec(memory_space=pl.ANY if i in any_out else VMEM) for i in range(len(outs))]
    out_shape = [
        jax.ShapeDtypeStruct(s, t) if i in any_out else VMEM(s, t) for i, (s, t) in enumerate(outs)
    ]
    ins = [pltpu.with_memory_space_constraint(x, pltpu.HBM if i in hbm else VMEM) for i, x in enumerate(ins)]
    return pl.pallas_call(
        kernel,
        in_specs=specs,
        out_specs=out_specs,
        out_shape=out_shape,
        scratch_shapes=list(scratch),
        compiler_params=pltpu.CompilerParams(vmem_limit_bytes=LIMIT),
        cost_estimate=cost,
        name=name,
    )(*ins)


def solution(mesh):
    across, along = mesh.shape["gx"], mesh.shape["gy"]

    def swap(x, first):
        def partner(i):
            return i ^ 1 if first else (i + 1 if i % 2 else i - 1) % across

        return lax.ppermute(x, "gx", [(i, partner(i)) for i in range(across)])

    def on_device(gradient, vertical, kernel):
        width, rows, cols = gradient.shape
        plan = Plan(rows, cols)
        parts = rows // PART
        n1, c1 = plan.counts[1]
        n2, c2 = plan.counts[2]
        size = rows * cols
        row_message = ((plan.row_size, width), BF16)
        cells = plan.cells
        raw, send_a, send_b, column, to_level1, to_level2 = call(
            lambda *refs: first_kernel(plan, *refs),
            [gradient],
            [
                ((parts, width, PART, cols), BF16), row_message, row_message,
                ((cells, size), BF16), ((9 * cols, 4 * c1), BF16), ((n1 * c1, n2 * c2), BF16),
            ],
            [
                VMEM((CHUNKS, 2, width // CHUNKS * PART, cols), F32),
                VMEM((2, width, 3 * cols), BF16), VMEM((plan.row_size, 3 * cols), BF16),
                pltpu.SemaphoreType.DMA((2 * CHUNKS + parts - 2,)),
            ],
            hbm=(0,),
            name="first",
        )
        recv_b = swap(send_b, False)
        recv_a = swap(send_a, True)
        flat, own, level1, level2 = call(
            lambda *refs: inner_kernel(plan, *refs),
            [raw, column, to_level1, to_level2],
            [
                ((width, size), BF16), ((cells, width), F32), ((width, n1 * c1), BF16),
                ((width, n2 * c2), BF16),
            ],
            [VMEM((parts, width * PART, cols), F32)],
            name="inner",
            cost=pl.CostEstimate(flops=3 * cells * width * size, bytes_accessed=4 * 1024 * 1024, transcendentals=0),
        )
        steps = routes(along)
        message = ((plan.message, width), BF16)
        right, *messages = call(
            lambda *refs: merge_kernel(plan, along, *refs),
            [own, recv_a, recv_b, const(plan.merge)],
            [message] * (1 + len(steps)),
            name="merge",
        )
        arrived = [lax.ppermute(x, "gy", list(enumerate(step))) for x, step in zip(messages, steps)]
        base, spread = call(
            lambda *refs: local_kernel(plan, along, *refs),
            [
                flat, level1, level2, to_level2, vertical, kernel, send_a, send_b, recv_a, recv_b, const(plan.even),
                const(plan.odd), const(plan.from_first), const(plan.from_last),
            ],
            [((width, size), F32), ((along * plan.cells3, 2 * plan.block), BF16)],
            [VMEM((width, n1 * c1), BF16)],
            name="local",
            cost=pl.CostEstimate(flops=4 * width * width * size, bytes_accessed=8 * 1024 * 1024, transcendentals=0),
        )
        (partial,) = call(
            lambda *refs: gather_kernel(plan, along, *refs),
            [right, *arrived[:-1], vertical, spread],
            [((width, plan.final_size), F32)],
            name="gather",
        )
        (out,) = call(
            lambda *refs: last_kernel(plan, along, *refs),
            [arrived[-1], partial, vertical, spread, const(plan.final), base],
            [((width, rows, cols), BF16)],
            [
                VMEM((parts, width * PART, cols), F32),
                VMEM((parts, width, PART, cols), BF16),
                pltpu.SemaphoreType.DMA((parts + CHUNKS - 1,)),
            ],
            any_out=(0,),
            name="last",
        )
        return out

    spec = P(None, "gx", "gy")
    return jax.shard_map(on_device, mesh=mesh, in_specs=(spec, P(), P()), out_specs=spec, check_vma=False)
```

```python
import jax
import jax.numpy as jnp
import ml_dtypes
import numpy as np
from jax import lax
from jax.experimental import pallas as pl
from jax.experimental.pallas import tpu as pltpu
from jax.sharding import PartitionSpec as P

BF16 = jnp.bfloat16
F32 = jnp.float32
PART = 8
CHUNKS = 2
VMEM = pltpu.VMEM


def hat(level, fine, cell):
    size = 2**level
    return np.maximum(0.0, 1.0 - np.abs(fine - size * cell) / size)


def weights(level, xs, ys, cell_x, cell_y):
    wx = hat(level, np.asarray(xs)[:, None], np.asarray(cell_x)[None, :])
    wy = hat(level, np.asarray(ys)[:, None], np.asarray(cell_y)[None, :])
    return (wx[:, None, :] * wy[None, :, :]).reshape(len(xs) * len(ys), len(cell_x))


def routes(count):
    if count == 4:
        return [(2, 3, 1, 0), (3, 2, 0, 1), (1, 0, 3, 2)]
    return [[(i + d) % count for i in range(count)] for d in range(1, count)]


def arrivals(count):
    return [
        [(k, step.index(z)) for k, step in enumerate(routes(count)) if step[z] != z] for z in range(count)
    ]


def chosen(index, values):
    result = index * 0
    for i, value in enumerate(values):
        result = result + jnp.where(index == i, value, 0)
    return result


def up16(n):
    return -(-n // 16) * 16


class Plan:
    def __init__(self, rows, cols):
        self.rows, self.cols = rows, cols
        ys = range(cols)
        counts = [(rows >> k, cols >> k) for k in range(4)]
        self.counts = counts
        row_cells = [(k, c) for k in (1, 2, 3) for c in range(counts[k][1] + 1)]
        self.row_cells = row_cells
        self.row_size = up16(len(row_cells))
        assert self.row_size == 128
        n3, m3 = counts[3][0] + 1, counts[3][1] + 1
        self.cells3 = up16(n3 * m3)
        self.block = -(-n3 * m3 // 128) * 128
        self.edge = (n3 * m3) // 16 * 16
        self.spare = n3 * m3 - self.edge
        level3 = [(3, r, c) for r in range(n3) for c in range(m3)]
        edge = [(k, r) for k in (1, 2) for r in range(counts[k][0] + 1)]
        self.message = up16(len(level3) + len(edge))
        self.edge_size = self.message - self.edge
        cells = []
        for side in (1, 0):
            part = [(k, r, side * counts[k][1]) for k, r in edge]
            part = (level3[self.edge :] if side else [None] * self.spare) + part
            cells += (level3[: self.edge] if side else []) + part + [None] * (self.edge_size - len(part))
        cells += [None] * (-len(cells) % 16)
        self.cells = len(cells)

        def table(cells, xs):
            out = np.zeros((len(cells), len(xs) * cols))
            for k in (1, 2, 3):
                where = [i for i, cell in enumerate(cells) if cell is not None and cell[0] == k]
                at = [cells[i] for i in where]
                out[where] = weights(k, xs, ys, [c[1] for c in at], [c[2] for c in at]).T
            return out

        self.cell_list = cells
        merge = np.zeros((len(cells), 2 * self.row_size))
        for i, cell in enumerate(cells):
            if cell is None:
                continue
            k, r, c = cell
            if r == 0:
                merge[i, row_cells.index((k, c))] = 1
            if r == counts[k][0]:
                merge[i, self.row_size + row_cells.index((k, c))] = 1
        self.merge = merge
        c1 = counts[1][1]
        grid = lambda n, m: (np.repeat(np.arange(n), m), np.tile(np.arange(m), n))
        self.even = weights(1, range(0, 2), ys, *grid(2, c1)).T
        self.odd = weights(1, range(2, 4), ys, *grid(4, c1)).T
        def from_row(xs, ends):
            out = np.zeros((2 * self.row_size, 4 * cols))
            for i, (k, c) in enumerate(row_cells):
                if k < 3 and c < counts[k][1]:
                    out[(k - 1) * self.row_size + i] = weights(k, xs, ys, [ends[k]], [c])[:, 0]
            return out

        self.from_first = from_row(range(0, 4), (0, 0, 0))
        self.from_last = from_row(range(rows - 4, rows), [n for n, _ in counts])
        final = [c for c in level3] + [None] * (self.block - len(level3))
        for k in (1, 2):
            for side in (0, 1):
                part = [None] * self.spare
                for level, r in edge:
                    part.append((k, r, side * counts[k][1]) if level == k else None)
                final += part + [None] * (self.edge_size - len(part))
        self.final_size = len(final)
        self.final = table(final, range(rows))


def const(table):
    return jnp.asarray(np.asarray(table).astype(ml_dtypes.bfloat16))


def dot(a, b):
    return jnp.dot(a, b, preferred_element_type=F32)


def dot_nt(a, b):
    return lax.dot_general(a, b, (((1,), (1,)), ((), ())), preferred_element_type=F32)


def ramp(size, offset):
    return jnp.maximum(0, size - jnp.abs(offset))


def cell_tables(cells, shape):
    index = lax.broadcasted_iota(jnp.int32, shape, 0)
    width, first, second = index * 0, index * 0, index * 0
    at = 0
    while at < len(cells):
        if cells[at] is None:
            at += 1
            continue
        k, r, c = cells[at]
        stop = at + 1
        step = None
        while stop < len(cells) and cells[stop] is not None and cells[stop][0] == k:
            move = (cells[stop][1] - cells[stop - 1][1], cells[stop][2] - cells[stop - 1][2])
            if step is None and move in ((0, 1), (1, 0)):
                step = move
            if move != step:
                break
            stop += 1
        step = step or (0, 0)
        mine = (index >= at) & (index < stop)
        width = jnp.where(mine, 2**k, width)
        first = jnp.where(mine, r + step[0] * (index - at), first)
        second = jnp.where(mine, c + step[1] * (index - at), second)
        at = stop
    return width, first, second


def split(index, size, count):
    high = index * 0
    for i in range(1, count):
        high = high + jnp.where(index >= i * size, 1, 0)
    return high, index - high * size


def first_kernel(plan, x_ref, raw_ref, a_ref, b_ref, column_ref, t1_ref, t2_ref, nat, sums, table, sem):
    rows, cols = plan.rows, plan.cols
    width = x_ref.shape[0]
    last = rows // PART - 1
    chunk = width // CHUNKS

    def fetch(h, start, count, i):
        fields = pl.ds(start, count)
        return pltpu.make_async_copy(x_ref.at[fields, pl.ds(h * PART, PART), :], raw_ref.at[h, fields], sem.at[i])

    copies = [
        [fetch(h, c * chunk, chunk, 2 * c + place) for place, h in enumerate((0, last))] for c in range(CHUNKS)
    ]
    copies.append([fetch(h, 0, width, 2 * CHUNKS + h - 1) for h in range(1, last)])
    for group in copies:
        for copy in group:
            copy.start()
    even = lax.rem(lax.axis_index("gx"), 2) == 0

    shape = (plan.cells, cols)
    size, first, second = cell_tables(plan.cell_list, shape)
    y = lax.broadcasted_iota(jnp.int32, shape, 1)
    inverse = jnp.where(size == 2, 0.25, jnp.where(size == 4, 0.0625, 0.015625))
    along = ramp(size, y - size * second).astype(F32) * inverse
    size, start = size.astype(F32), (size * first).astype(F32)
    for x in range(rows):
        column_ref[:, pl.ds(x * cols, cols)] = (ramp(size, start - x) * along).astype(BF16)
    n1, c1 = plan.counts[1]
    n2, c2 = plan.counts[2]
    shape = (cols, 4 * c1)
    i, c = split(lax.broadcasted_iota(jnp.int32, shape, 1), c1, 4)
    along = ramp(2, lax.broadcasted_iota(jnp.int32, shape, 0) - 2 * c).astype(F32) * 0.25
    i = 2 * i[:1]
    for x in range(9):
        t1_ref[pl.ds(x * cols, cols), :] = (ramp(2, i - (x - 1)).astype(F32) * along).astype(BF16)
    shape = (c1, n2 * c2)
    i, c = split(lax.broadcasted_iota(jnp.int32, shape, 1), c2, n2)
    along = ramp(2, lax.broadcasted_iota(jnp.int32, shape, 0) - 2 * c).astype(F32) * 0.25
    i = 2 * i[:1]
    for x in range(n1):
        t2_ref[pl.ds(x * c1, c1), :] = (ramp(2, i - x).astype(F32) * along).astype(BF16)
    shape = (plan.row_size, cols)
    level, _, second = cell_tables([(k, 0, c) for k, c in plan.row_cells], shape)
    y = lax.broadcasted_iota(jnp.int32, shape, 1)
    for k in (1, 2, 3):
        weight = ramp(2**k, y - 2**k * second).astype(F32) * 0.5**k
        table[:, pl.ds((k - 1) * cols, cols)] = jnp.where(level == 2**k, weight, 0.0).astype(BF16)
    for c in range(CHUNKS):
        fields = pl.ds(c * chunk, chunk)
        for place, (h, end) in enumerate(((0, 0), (last, PART))):
            copies[c][place].wait()
            nat[c, place] = raw_ref[h, fields].astype(F32).reshape(chunk * PART, cols)
            found = [None] * 3
            for x in range(PART):
                row = nat[c, place, pl.ds(x, chunk, stride=PART), :]
                for k in range(3):
                    weight = float(hat(k + 1, x, end / 2 ** (k + 1)))
                    if weight:
                        term = row * weight
                        found[k] = term if found[k] is None else found[k] + term
            for k in range(3):
                sums[place, fields, pl.ds(k * cols, cols)] = found[k].astype(BF16)
    low, up = [dot_nt(table[...], sums[place]).astype(BF16) for place in range(2)]
    a_ref[...] = jnp.where(even, up, low)
    b_ref[...] = jnp.where(even, low, up)
    for copy in copies[-1]:
        copy.wait()


def inner_kernel(
    plan, raw_ref, column_ref, t1_ref, t2_ref, flat_ref, own_ref, level1, level2, nat
):
    rows, cols = plan.rows, plan.cols
    width = raw_ref.shape[1]
    for h in range(rows // PART):
        nat[h] = raw_ref[h].astype(F32).reshape(width * PART, cols)
        for x in range(PART):
            row = nat[h, pl.ds(x, width, stride=PART), :]
            flat_ref[:, pl.ds((h * PART + x) * cols, cols)] = row.astype(BF16)

    def fine(x, count):
        return flat_ref[:, pl.ds(x * cols, count * cols)]

    total = None
    for x in range(0, rows, 2):
        term = dot_nt(column_ref[:, pl.ds(x * cols, 2 * cols)], fine(x, 2))
        total = term if total is None else total + term
    own_ref[...] = total
    n1, c1 = plan.counts[1]
    for k in range(rows // 8):
        total = None
        for j in range(4):
            term = dot(fine(8 * k + 2 * j, 2), t1_ref[pl.ds((2 * j + 1) * cols, 2 * cols), :])
            total = term if total is None else total + term
        if k > 0:
            total = total + dot(fine(8 * k - 1, 1), t1_ref[pl.ds(0, cols), :])
        level1[:, pl.ds(4 * k * c1, 4 * c1)] = (total * (1 / 1.5)).astype(BF16)
    level2[...] = (dot(level1[...], t2_ref[...]) * (1 / 1.5)).astype(BF16)


def merge_kernel(plan, count, own_ref, b_ref, a_ref, merge_ref, right_ref, *out_refs):
    even = lax.rem(lax.axis_index("gx"), 2) == 0
    a, b = a_ref[...], b_ref[...]
    before, after = jnp.where(even, b, a), jnp.where(even, a, b)
    total32 = own_ref[...] + dot(merge_ref[...], jnp.concatenate([before, after], axis=0))
    total = total32.astype(BF16)
    right_ref[...] = total[: plan.message]
    row = lax.broadcasted_iota(jnp.int32, (plan.edge_size, total.shape[1]), 0)
    tile = jnp.where(row < plan.spare, total32[plan.edge : plan.message], total32[plan.message :])
    right, left = total[plan.edge : plan.message], tile.astype(BF16)
    z = lax.axis_index("gy")
    for step, ref in zip(routes(count), out_refs):
        to_left = chosen(z, [int(step[i] == i - 1) for i in range(count)]) == 1
        ref[: plan.edge] = total[: plan.edge]
        ref[plan.edge :] = jnp.where(to_left, left, right)


def source_of(z, count, d):
    return z if d == 0 else chosen(z, [got[d - 1][1] for got in arrivals(count)])


def local_kernel(
    plan, count, flat_ref, level1, level2, t2_ref, v_ref, k_ref, sa_ref, sb_ref, ra_ref, rb_ref, even_ref, odd_ref,
    first_ref, last_ref, base_ref, spread_ref, carry1,
):
    rows, cols = plan.rows, plan.cols
    n1, c1 = plan.counts[1]
    mixed2 = (dot(v_ref[2], level2[...]) * (1 / 1.5)).astype(BF16)
    step = 4 * c1
    for k in range(n1 * c1 // step):
        lanes = pl.ds(k * step, step)
        mixed1 = dot(v_ref[1], level1[:, lanes]) + dot_nt(mixed2, t2_ref[lanes, :])
        carry1[:, lanes] = (mixed1 * (1 / 1.5)).astype(BF16)

    even = lax.rem(lax.axis_index("gx"), 2) == 0
    a, b = ra_ref[...], rb_ref[...]
    before, after = jnp.where(even, b, a), jnp.where(even, a, b)
    own = jnp.where(even, sa_ref[...], sb_ref[...])
    after = (after.astype(F32) + own.astype(F32)).astype(BF16)

    def mixed_rows(message):
        one = dot_nt(v_ref[1], message) * (1 / 1.5**2)
        two = dot_nt(v_ref[2], message) * (1 / 1.5**4)
        return jnp.concatenate([one, two], axis=1).astype(BF16)

    first, last = mixed_rows(before), mixed_rows(after)
    pairs = rows // 2
    for i in range(pairs):
        lanes = pl.ds(2 * i * cols, 2 * cols)
        total = dot(v_ref[0], flat_ref[:, lanes])
        if i % 2 == 0:
            total = total + dot(carry1[:, pl.ds(i * c1, 2 * c1)], even_ref[...])
        elif i < pairs - 1:
            total = total + dot(carry1[:, pl.ds((i - 1) * c1, 4 * c1)], odd_ref[...])
        else:
            total = total + dot(carry1[:, pl.ds((i - 1) * c1, 2 * c1)], odd_ref[pl.ds(0, 2 * c1), :])
        if i < 2:
            total = total + dot(first, first_ref[:, pl.ds(2 * i * cols, 2 * cols)])
        if i >= pairs - 2:
            total = total + dot(last, last_ref[:, pl.ds(2 * (i - pairs + 2) * cols, 2 * cols)])
        base_ref[:, lanes] = total

    n3, m3 = plan.counts[3][0] + 1, plan.counts[3][1] + 1
    size = k_ref.shape[0]
    block, cells3 = plan.block, plan.cells3
    z = lax.axis_index("gy")

    def parts(shape, dim):
        index = lax.broadcasted_iota(jnp.int32, shape, dim)
        row = jnp.zeros(shape, jnp.int32)
        for r in range(1, n3 + 1):
            row = row + jnp.where(index >= r * m3, 1, 0)
        return row, index - row * m3

    def one(mask):
        return jnp.where(mask, 1.0, 0.0).astype(BF16)

    row, col = parts((size, block), 1)
    place = lax.broadcasted_iota(jnp.int32, (size, block), 0)
    picked = dot(k_ref[...], one((place == z * (m3 - 1) + col) & (row < n3))).astype(BF16)
    source_row, source_col = parts((cells3, block), 0)
    target_row, target_col = parts((cells3, block), 1)
    same = (target_row == source_row) & (target_row < n3)
    target = z * (m3 - 1) + target_col
    _, col = parts((cells3, size), 0)
    place = lax.broadcasted_iota(jnp.int32, (cells3, size), 1)
    for d in range(count):
        start = source_of(z, count, d) * (m3 - 1)
        spread = jnp.where(same, dot(one(place == start + col), picked), 0.0).astype(BF16)
        keep = one(same & (target == start + source_col) & (target < size))
        spread_ref[pl.ds(d * cells3, cells3), :block] = spread
        spread_ref[pl.ds(d * cells3, cells3), block:] = keep


def column_parts(plan, count, messages, first, v_ref, spread_ref):
    width = v_ref.shape[1]
    block, cells3 = plan.block, plan.cells3
    z = lax.axis_index("gy")
    level3 = jnp.concatenate([message[:cells3] for message in messages], axis=0)
    mixed = (dot_nt(v_ref[3], level3) * (1 / 1.5**3)).astype(BF16)
    carry = dot(mixed, spread_ref[pl.ds(first * cells3, len(messages) * cells3), :])
    carry = (carry[:, :block] + carry[:, block:]) * (1 / 1.5**3)
    left = jnp.zeros((plan.edge_size, width), F32)
    right = jnp.zeros((plan.edge_size, width), F32)
    for d, message in enumerate(messages, first):
        source, edge = source_of(z, count, d), message[plan.edge :].astype(F32)
        if d == 0:
            right = right + edge
        else:
            left = left + jnp.where((source == z - 1) & (z > 0), edge, 0.0)
            right = right + jnp.where(source == z + 1, edge, 0.0)
    right = jnp.where(z < count - 1, right, 0.0)
    edges = jnp.concatenate([left, right], axis=0).astype(BF16)
    one = dot_nt(v_ref[1], edges) * (1 / 1.5**2)
    two = dot_nt(v_ref[2], edges) * (1 / 1.5**4)
    return jnp.concatenate([carry, one, two], axis=1)


def gather_kernel(plan, count, *refs):
    *message_refs, v_ref, spread_ref, parts_ref = refs
    parts_ref[...] = column_parts(plan, count, [ref[...] for ref in message_refs], 0, v_ref, spread_ref)


def last_kernel(plan, count, in_ref, parts_ref, v_ref, spread_ref, final_ref, base_ref, out_ref, nat, buf, sem):
    rows, cols = plan.rows, plan.cols
    width = v_ref.shape[1]
    parts = column_parts(plan, count, [in_ref[...]], count - 1, v_ref, spread_ref)
    parts = (parts + parts_ref[...]).astype(BF16)
    copies = []
    for h in range(rows // PART):
        lanes = pl.ds(h * PART * cols, PART * cols)
        total = base_ref[:, lanes] + dot(parts, final_ref[:, lanes])
        for x in range(PART):
            nat[h, pl.ds(x, width, stride=PART), :] = total[:, x * cols : (x + 1) * cols]
        pieces = CHUNKS if h == rows // PART - 1 else 1
        part = width // pieces
        for i in range(pieces):
            fields = pl.ds(i * part, part)
            found = nat[h, pl.ds(i * part * PART, part * PART), :]
            buf[h, fields] = found.reshape(part, PART, cols).astype(BF16)
            copy = pltpu.make_async_copy(
                buf.at[h, fields], out_ref.at[fields, pl.ds(h * PART, PART), :], sem.at[h + i]
            )
            copy.start()
            copies.append(copy)
    for copy in copies:
        copy.wait()


LIMIT = 14 * 1024 * 1024


def call(kernel, ins, outs, scratch=(), hbm=(), any_out=(), name=None, cost=None):
    specs = [pl.BlockSpec(memory_space=pl.ANY if i in hbm else VMEM) for i in range(len(ins))]
    out_specs = [pl.BlockSpec(memory_space=pl.ANY if i in any_out else VMEM) for i in range(len(outs))]
    out_shape = [
        jax.ShapeDtypeStruct(s, t) if i in any_out else VMEM(s, t) for i, (s, t) in enumerate(outs)
    ]
    ins = [pltpu.with_memory_space_constraint(x, pltpu.HBM if i in hbm else VMEM) for i, x in enumerate(ins)]
    return pl.pallas_call(
        kernel,
        in_specs=specs,
        out_specs=out_specs,
        out_shape=out_shape,
        scratch_shapes=list(scratch),
        compiler_params=pltpu.CompilerParams(vmem_limit_bytes=LIMIT),
        cost_estimate=cost,
        name=name,
    )(*ins)


def solution(mesh):
    across, along = mesh.shape["gx"], mesh.shape["gy"]

    def swap(x, first):
        def partner(i):
            return i ^ 1 if first else (i + 1 if i % 2 else i - 1) % across

        return lax.ppermute(x, "gx", [(i, partner(i)) for i in range(across)])

    def on_device(gradient, vertical, kernel):
        width, rows, cols = gradient.shape
        plan = Plan(rows, cols)
        parts = rows // PART
        n1, c1 = plan.counts[1]
        n2, c2 = plan.counts[2]
        size = rows * cols
        row_message = ((plan.row_size, width), BF16)
        cells = plan.cells
        raw, send_a, send_b, column, to_level1, to_level2 = call(
            lambda *refs: first_kernel(plan, *refs),
            [gradient],
            [
                ((parts, width, PART, cols), BF16), row_message, row_message,
                ((cells, size), BF16), ((9 * cols, 4 * c1), BF16), ((n1 * c1, n2 * c2), BF16),
            ],
            [
                VMEM((CHUNKS, 2, width // CHUNKS * PART, cols), F32),
                VMEM((2, width, 3 * cols), BF16), VMEM((plan.row_size, 3 * cols), BF16),
                pltpu.SemaphoreType.DMA((2 * CHUNKS + parts - 2,)),
            ],
            hbm=(0,),
            name="first",
        )
        recv_b = swap(send_b, False)
        recv_a = swap(send_a, True)
        flat, own, level1, level2 = call(
            lambda *refs: inner_kernel(plan, *refs),
            [raw, column, to_level1, to_level2],
            [
                ((width, size), BF16), ((cells, width), F32), ((width, n1 * c1), BF16),
                ((width, n2 * c2), BF16),
            ],
            [VMEM((parts, width * PART, cols), F32)],
            name="inner",
            cost=pl.CostEstimate(flops=3 * cells * width * size, bytes_accessed=4 * 1024 * 1024, transcendentals=0),
        )
        steps = routes(along)
        message = ((plan.message, width), BF16)
        right, *messages = call(
            lambda *refs: merge_kernel(plan, along, *refs),
            [own, recv_b, recv_a, const(plan.merge)],
            [message] * (1 + len(steps)),
            name="merge",
        )
        arrived = [lax.ppermute(x, "gy", list(enumerate(step))) for x, step in zip(messages, steps)]
        base, spread = call(
            lambda *refs: local_kernel(plan, along, *refs),
            [
                flat, level1, level2, to_level2, vertical, kernel, send_a, send_b, recv_a, recv_b, const(plan.even),
                const(plan.odd), const(plan.from_first), const(plan.from_last),
            ],
            [((width, size), F32), ((along * plan.cells3, 2 * plan.block), BF16)],
            [VMEM((width, n1 * c1), BF16)],
            name="local",
            cost=pl.CostEstimate(flops=4 * width * width * size, bytes_accessed=8 * 1024 * 1024, transcendentals=0),
        )
        (partial,) = call(
            lambda *refs: gather_kernel(plan, along, *refs),
            [right, *arrived[:-1], vertical, spread],
            [((width, plan.final_size), F32)],
            name="gather",
        )
        (out,) = call(
            lambda *refs: last_kernel(plan, along, *refs),
            [arrived[-1], partial, vertical, spread, const(plan.final), base],
            [((width, rows, cols), BF16)],
            [
                VMEM((parts, width * PART, cols), F32),
                VMEM((parts, width, PART, cols), BF16),
                pltpu.SemaphoreType.DMA((parts + CHUNKS - 1,)),
            ],
            any_out=(0,),
            name="last",
        )
        return out

    spec = P(None, "gx", "gy")
    return jax.shard_map(on_device, mesh=mesh, in_specs=(spec, P(), P()), out_specs=spec, check_vma=False)
```
